32 devices in a mesh: rep: 8 (over z, x), tp: 4 (over y, core).
Axes of the slice: x: 2, y: 2, z: 4, core: 2. Of those that a mesh axis runs over, the one named last changes fastest.
Arguments:
- tokens: bfloat16 [1024, 1024], P('rep', 'tp'), may hold values from -6 to 6
- attn_gain: float32 [1024], replicated, may hold values from 0.1 to 1.9
- ffn_gain: float32 [1024], replicated, may hold values from 0.1 to 1.9
- w_query: bfloat16 [1024, 1024], P(None, 'tp'), may hold values from -0.0625 to 0.0625
- w_key: bfloat16 [1024, 1024], P(None, 'tp'), may hold values from -0.1875 to 0.1875
- w_value: bfloat16 [1024, 1024], P(None, 'tp'), may hold values from -0.1875 to 0.1875
- w_out: bfloat16 [1024, 1024], P('tp'), may hold values from -0.1875 to 0.1875
- w_inner: bfloat16 [1024, 2048], P(None, 'tp'), may hold values from -0.1875 to 0.1875
- w_outer: bfloat16 [2048, 1024], P('tp'), may hold values from -0.125 to 0.125
- bias_table: float32 [32, 16], P(None, 'tp'), may hold values from -3 to 3
- cache_keys: bfloat16 [16, 64, 1024], P('rep', None, 'tp'), may hold values from -68 to 68
- cache_values: bfloat16 [16, 64, 1024], P('rep', None, 'tp'), may hold values from -6 to 6
- new_counts: int32 [2, 8], P(None, 'rep'), may hold values from 1 to 64, 256 in all within a row
- cached_lengths: int32 [2, 8], P(None, 'rep'), may hold values from 1 to 64, 256 in all within a row
- deal: int32 [8, 128], P('rep'), may hold values from 0 to 127, each once within a row
Outputs:
- dealt: bfloat16 [1024, 1024], P('rep', 'tp')
The draws below stay inside these ranges and needn't reach their ends.
Inputs may be any that keep to these rules, and one draw needn't show every extreme that they name: `new_counts`: for each j the counts over the replicas sum to 256. `cached_lengths`: for each j the lengths over the replicas sum to 256. `deal`: each row holds every number of 0 to 127 once.
All inputs are finite; a program needn't handle non-finite values. No bound on the sum of `new_counts` or of `cached_lengths` on one device may be relied on, other than what follows from the above.
Results may differ from the reference program's by a relative error of at most 0.013.
The reference program's roundings to bfloat16 on the way (of `normed`, `attn_probs`, `context`, `ffn_input`, `hidden` and `layer_out`) count: a program that leaves them out, or rounds other values in their place, can miss the bound.
Values may be sent and summed in bfloat16 or wider, within the bound.
No kernel may reach another device: no remote copies, remote signals or barrier semaphores. Data moves between devices by JAX's collectives and lax.ppermute only.
A program may use at most 64 MiB of HBM per device.

```python
import math
import jax
import jax.numpy as jnp
import numpy as np
from jax import lax

D = 1024
HEADS = 16
HDIM = 64
FF = 2048
BUCKETS = 32
REQ_DEV = 2
QLEN = 64
CLEN = 64
TOK_DEV = 128
REQS = 16
TOKENS = 1024
N_REP = 8


def draw_cache_keys(key, part):
    first = jax.random.fold_in(key, 0)
    base = jnp.clip(jax.random.normal(first, (REQS, CLEN, D), jnp.float32), -4.0, 4.0)
    return base.astype(jnp.bfloat16)


def steps_of(rng, extent, pieces, low, top_value):
    def one(axis_at, blocks):
        draws = jax.random.uniform(jax.random.fold_in(jax.random.fold_in(rng, 6), axis_at), (blocks,), jnp.float32, low / len(pieces), top_value / len(pieces))
        return jnp.repeat(jnp.exp(draws), extent[axis_at] // blocks).reshape((-1,) + (1,) * (len(extent) - axis_at - 1))

    gain = one(*pieces[0])
    for cut in pieces[1:]:
        gain = gain * one(*cut)
    return gain


def split_up(amount, total, bound, skew):
    loads = [(1 << 20) // math.isqrt(rank ** skew) + 1 for rank in range(2, amount + 1)]
    spare, holding = total - bound - (amount - 1), [1] * (amount - 1)
    while spare > 0:
        free = [i for i in range(amount - 1) if holding[i] < bound]
        pool, budget = sum([loads[i] for i in free]), spare
        for i in free:
            more = min(bound - holding[i], max(1, budget * loads[i] // pool), spare)
            holding[i] = holding[i] + more
            spare = spare - more
    return np.array([bound] + holding)


def uneven(key, amount, total, limit, skew):
    if amount == 2:
        one = jax.random.randint(key, (), max(1, total - limit), min(limit, total - 1) + 1)
        return jnp.stack([one, total - one])
    tallies = jnp.asarray(split_up(amount, total, limit, skew), jnp.int32)
    couples = (amount - 1) // 2
    source_of, sink = tallies[1:1 + 2 * couples:2], tallies[2:2 + 2 * couples:2]
    margin = jnp.minimum(source_of - 1, limit - sink)
    shifted = jax.random.randint(jax.random.fold_in(key, 1), (couples,), 0, 1 << 20) % (margin + 1)
    tallies = tallies.at[1:1 + 2 * couples:2].set(source_of - shifted).at[2:2 + 2 * couples:2].set(sink + shifted)
    return tallies[jax.random.permutation(jax.random.fold_in(key, 2), amount)]


def gaussian(key, extent, spread, reach, cuts=(), held_as=jnp.bfloat16):
    gain = steps_of(key, extent, cuts, -0.22, 0.18) if cuts else 1.0
    entries = jax.random.normal(key, extent, jnp.float32) * spread * gain
    return jnp.minimum(jnp.maximum(entries, -reach), reach).astype(held_as)


def setup_inputs(seed: int = 0) -> dict:
    keys = jax.random.split(jax.random.key(seed), 16)
    tokens = gaussian(keys[0], (TOKENS, D), 1.0, 6.0, ((0, 8), (1, 4)))
    attn_gain = jnp.clip(1.0 + 0.18 * jax.random.normal(keys[1], (D,), jnp.float32), 0.1, 1.9)
    ffn_gain = jnp.clip(1.0 + 0.18 * jax.random.normal(keys[2], (D,), jnp.float32), 0.1, 1.9)
    w_query = gaussian(keys[3], (D, D), (8 * D) ** -0.5, 0.0625, ((1, 4),))
    w_key = gaussian(keys[4], (D, D), D ** -0.5, 0.1875, ((1, 4),))
    w_value = gaussian(keys[5], (D, D), D ** -0.5, 0.1875, ((1, 4),))
    w_out = gaussian(keys[6], (D, D), D ** -0.5, 0.1875, ((0, 4),))
    w_inner = gaussian(keys[7], (D, FF), D ** -0.5, 0.1875, ((1, 4),))
    w_outer = gaussian(keys[8], (FF, D), FF ** -0.5, 0.125, ((0, 4),))
    bias_table = jnp.clip(jax.random.uniform(keys[9], (BUCKETS, HEADS), jnp.float32, -3.0, 3.0) * steps_of(keys[9], (BUCKETS, HEADS), ((1, 4),), -0.4, 0.0), -3.0, 3.0)
    cache_keys = draw_cache_keys(jax.random.fold_in(keys[15], 71), 0)
    cache_values = gaussian(keys[11], (REQS, CLEN, D), 1.0, 6.0, ((0, 8), (2, 4)))
    new_counts = jax.vmap(lambda own: uneven(own, N_REP, N_REP * QLEN // 2, QLEN, 2))(jax.random.split(keys[12], REQ_DEV)).reshape((REQ_DEV, N_REP)).astype(jnp.int32)
    cached_lengths = jax.vmap(lambda own: uneven(own, N_REP, N_REP * CLEN // 2, CLEN, 2))(jax.random.split(keys[13], REQ_DEV)).reshape((REQ_DEV, N_REP)).astype(jnp.int32)
    deal = jax.vmap(lambda own: jax.random.permutation(own, TOK_DEV))(jax.random.split(keys[14], N_REP)).reshape((N_REP, TOK_DEV)).astype(jnp.int32)
    return dict(tokens=tokens, attn_gain=attn_gain, ffn_gain=ffn_gain, w_query=w_query, w_key=w_key, w_value=w_value, w_out=w_out, w_inner=w_inner, w_outer=w_outer, bias_table=bias_table, cache_keys=cache_keys, cache_values=cache_values, new_counts=new_counts, cached_lengths=cached_lengths, deal=deal)


EPSILON = 1e-06
THRESHOLDS = (12, 16, 23, 32, 46, 64, 91)

def bucket_of(relative):
    distance = jnp.abs(relative)
    larger = 8 + sum(((distance >= threshold).astype(jnp.int32) for threshold in THRESHOLDS))
    near = jnp.where(distance < 8, distance, larger)
    return near + 16 * (relative > 0).astype(jnp.int32)

def rms_scale(values):
    return lax.rsqrt(lax.optimization_barrier(jnp.mean(values * values, axis=-1, keepdims=True)) + EPSILON)

def reference(tokens, attn_gain, ffn_gain, w_query, w_key, w_value, w_out, w_inner, w_outer, bias_table, cache_keys, cache_values, new_counts, cached_lengths, deal):
    stream = tokens.astype(jnp.float32)
    normed = (stream * rms_scale(stream) * attn_gain).astype(jnp.bfloat16)
    queries = jnp.dot(normed, w_query, preferred_element_type=jnp.float32).astype(jnp.bfloat16).reshape(REQS, QLEN, HEADS, HDIM)
    new_keys = jnp.dot(normed, w_key, preferred_element_type=jnp.float32).astype(jnp.bfloat16).reshape(REQS, QLEN, D)
    new_values = jnp.dot(normed, w_value, preferred_element_type=jnp.float32).astype(jnp.bfloat16).reshape(REQS, QLEN, D)
    counts = new_counts.T.reshape(REQS).astype(jnp.int32)
    lengths = cached_lengths.T.reshape(REQS).astype(jnp.int32)
    key_index = jnp.arange(CLEN + QLEN, dtype=jnp.int32)
    offsets = jnp.arange(QLEN, dtype=jnp.int32)
    per_head = bias_table.T

    def attend(item):
        query, cache_k, cache_v, fresh_k, fresh_v, count, length = item
        all_keys = jnp.concatenate([cache_k, fresh_k], axis=0).reshape(CLEN + QLEN, HEADS, HDIM).astype(jnp.float32)
        all_values = jnp.concatenate([cache_v, fresh_v], axis=0).reshape(CLEN + QLEN, HEADS, HDIM).astype(jnp.float32)
        scores = jnp.einsum('qhd,khd->hqk', query.astype(jnp.float32), all_keys)
        is_cache = key_index < CLEN
        key_position = jnp.where(is_cache, key_index, length + key_index - CLEN)
        relative = key_position[None, :] - (length + offsets)[:, None]
        rel_bias = jnp.take(per_head, bucket_of(relative), axis=1)
        live_key = jnp.where(is_cache, key_index < length, key_index - CLEN < count)
        scores = jnp.where(live_key[None, None, :], scores + rel_bias, -1e+30)
        row_max = lax.optimization_barrier(jnp.max(scores, axis=2, keepdims=True))
        weights = jnp.exp(scores - row_max)
        attn_probs = (weights / lax.optimization_barrier(jnp.sum(weights, axis=2, keepdims=True))).astype(jnp.bfloat16)
        context = jnp.einsum('hqk,khd->qhd', attn_probs.astype(jnp.float32), all_values)
        return context.astype(jnp.bfloat16).reshape(QLEN, D)
    context = lax.map(attend, (queries, cache_keys, cache_values, new_keys, new_values, counts, lengths)).reshape(TOKENS, D)
    mixed = stream + jnp.dot(context, w_out, preferred_element_type=jnp.float32)
    live_rows = (offsets[None, :] < counts[:, None]).reshape(TOKENS, 1)
    mixed = jnp.where(live_rows, mixed, 0.0)
    ffn_input = (mixed * rms_scale(mixed) * ffn_gain).astype(jnp.bfloat16)
    hidden = jnp.maximum(jnp.dot(ffn_input, w_inner, preferred_element_type=jnp.float32), 0.0).astype(jnp.bfloat16)
    layer_out = (mixed + jnp.dot(hidden, w_outer, preferred_element_type=jnp.float32)).astype(jnp.bfloat16)
    replicas = jnp.arange(N_REP, dtype=jnp.int32)
    target = deal % N_REP * TOK_DEV + replicas[:, None] * (TOK_DEV // N_REP) + deal // N_REP
    return jnp.zeros_like(layer_out).at[target.reshape(TOKENS)].set(layer_out)
```

```python
import functools

import jax
import jax.numpy as jnp
from jax import lax
from jax.experimental import pallas as pl
from jax.experimental.pallas import tpu as pltpu
from jax.sharding import Mesh, PartitionSpec as P

EPSILON = 1e-06
THRESHOLDS = (1, 2, 3, 4, 5, 6, 7, 8, 12, 16, 23, 32, 46, 64, 91)
BF16 = jnp.bfloat16
F32 = jnp.float32
VMEM = pl.BlockSpec(memory_space=pltpu.VMEM)
SMEM = pl.BlockSpec(memory_space=pltpu.SMEM)
VMEM_LIMIT = 24 * 1024 * 1024


def dot(a, b):
    return jnp.dot(a, b, preferred_element_type=F32)


def deal_matrix(deal, counts_ref, replicas, new_slots, half, core):
    rows = deal.shape[1]
    share = rows // replicas
    lane = lax.broadcasted_iota(jnp.int32, (1, rows), 1)
    live = jnp.zeros((1, rows), jnp.bool_)
    for j in range(rows // new_slots):
        offset = lane - j * new_slots
        live = live | ((offset >= 0) & (offset < jnp.minimum(counts_ref[j, 0], new_slots)))
    slot = lax.rem(deal, replicas) * share + lax.div(deal, replicas)
    slot = jnp.where(live, slot, -1)
    row = lax.broadcasted_iota(jnp.int32, (rows, rows), 0)
    row = jnp.where(core == 0, row, jnp.where(row < half, row + half, row - half))
    return jnp.where(row == slot, 1.0, 0.0).astype(BF16)


def bias_of(table_ref, relative, head):
    distance = jnp.abs(relative)
    before = jnp.full(relative.shape, table_ref[0, head], F32)
    after = jnp.full(relative.shape, table_ref[17, head], F32)
    for step, threshold in enumerate(THRESHOLDS):
        far = distance >= threshold
        before = jnp.where(far, table_ref[step + 1, head], before)
        after = jnp.where(far, table_ref[step + 17, head], after)
    return jnp.where(relative > 0, after, before)


def attend_kernel(
    replicas,
    x_ref,
    gain_ref,
    w_query_ref,
    w_key_ref,
    w_value_ref,
    w_out_ref,
    table_ref,
    cache_keys_ref,
    cache_values_ref,
    counts_ref,
    lengths_ref,
    deal_ref,
    keep_ref,
    send_ref,
):
    core = lax.axis_index("lo")
    blocks, rows, width = x_ref.shape
    model_width = blocks * width
    requests, cached, local_width = cache_keys_ref.shape
    new_slots = rows // requests
    head_count = table_ref.shape[1]
    head_size = local_width // head_count
    half = rows // 2

    squares = 0.0
    for b in range(blocks):
        block = x_ref[b].astype(F32)
        squares = squares + jnp.sum(block * block, axis=1, keepdims=True)
    inverse = lax.rsqrt(squares / model_width + EPSILON)
    normed = jnp.concatenate(
        [
            (x_ref[b].astype(F32) * inverse * gain_ref[:, b * width : (b + 1) * width]).astype(BF16)
            for b in range(blocks)
        ],
        axis=1,
    )
    queries = dot(normed, w_query_ref[...]).astype(BF16)
    new_keys = dot(normed, w_key_ref[...]).astype(BF16)
    new_values = dot(normed, w_value_ref[...]).astype(BF16)

    key_slots = cached + new_slots
    lane_head = lax.broadcasted_iota(jnp.int32, (new_slots, local_width), 1) // head_size
    key_index = lax.broadcasted_iota(jnp.int32, (new_slots, key_slots), 1)
    query_index = lax.broadcasted_iota(jnp.int32, (new_slots, key_slots), 0)
    is_cache = key_index < cached
    contexts = []
    for j in range(requests):
        own = slice(j * new_slots, (j + 1) * new_slots)
        length = lengths_ref[j, 0]
        count = counts_ref[j, 0]
        position = jnp.where(is_cache, key_index, length + key_index - cached)
        relative = position - (length + query_index)
        live = jnp.where(is_cache, key_index - length, key_index - cached - count) < 0
        query = queries[own]
        stacked = jnp.concatenate(
            [jnp.where(lane_head == h, query, jnp.zeros_like(query)) for h in range(head_count)],
            axis=0,
        )
        keys = jnp.concatenate([cache_keys_ref[j], new_keys[own]], axis=0)
        values = jnp.concatenate([cache_values_ref[j], new_values[own]], axis=0)
        scores = lax.dot_general(
            stacked, keys, (((1,), (1,)), ((), ())), preferred_element_type=F32
        )
        probs = []
        for h in range(head_count):
            score = scores[h * new_slots : (h + 1) * new_slots]
            score = jnp.where(live, score + bias_of(table_ref, relative, h), -1e30)
            weight = jnp.exp(score - jnp.max(score, axis=1, keepdims=True))
            probs.append((weight / jnp.sum(weight, axis=1, keepdims=True)).astype(BF16))
        mixed = dot(jnp.concatenate(probs, axis=0), values)
        context = jnp.zeros((new_slots, local_width), F32)
        for h in range(head_count):
            context = jnp.where(lane_head == h, mixed[h * new_slots : (h + 1) * new_slots], context)
        contexts.append(context.astype(BF16))
    picked = deal_matrix(deal_ref[...], counts_ref, replicas, new_slots, half, core)
    context = dot(picked, jnp.concatenate(contexts, axis=0)).astype(BF16)
    send_ref[...] = dot(context[half:], w_out_ref[...]).astype(BF16)
    keep_ref[...] = dot(context[:half], w_out_ref[...])


def stream_kernel(replicas, new_slots, x_ref, counts_ref, deal_ref, stream_ref):
    core = lax.axis_index("lo")
    blocks, rows, width = x_ref.shape
    picked = deal_matrix(deal_ref[...], counts_ref, replicas, new_slots, rows // 2, core)
    for b in range(blocks):
        stream_ref[:, b * width : (b + 1) * width] = dot(picked, x_ref[b]).astype(BF16)


def ffn_kernel(own_ref, other_ref, stream_ref, gain_ref, w_inner_ref, w_outer_ref, keep_ref, send_ref):
    core = lax.axis_index("lo")
    upper = lax.axis_index("hi")
    half, model_width = own_ref.shape
    groups, _, width = keep_ref.shape
    for part, ref in enumerate((own_ref, other_ref)):
        start = pl.multiple_of(lax.rem(core + part, 2) * half, half)
        mixed = ref[...].astype(F32) + stream_ref[part * half : (part + 1) * half].astype(F32)
        square = jnp.sum(mixed * mixed, axis=1, keepdims=True)
        inverse = lax.rsqrt(square / model_width + EPSILON)
        ffn_input = (mixed * inverse * gain_ref[...]).astype(BF16)
        hidden = jnp.maximum(dot(ffn_input, w_inner_ref[...]), 0.0).astype(BF16)
        projected = dot(hidden, w_outer_ref[...])
        for g in range(groups):
            for c in range(2):
                columns = slice((g * 2 + c) * width, (g * 2 + c + 1) * width)
                mine = (upper == g) & (core == c)
                value = projected[:, columns] + jnp.where(mine, mixed[:, columns], 0.0)

                @pl.when(core == c)
                def _():
                    keep_ref[g, pl.ds(start, half), :] = value

                @pl.when(core != c)
                def _():
                    send_ref[g, pl.ds(start, half), :] = value.astype(BF16)


def swap(value, axis):
    return lax.ppermute(value, axis, [(0, 1), (1, 0)])


def on_device(
    replicas,
    tokens,
    attn_gain,
    ffn_gain,
    w_query,
    w_key,
    w_value,
    w_out,
    w_inner,
    w_outer,
    bias_table,
    cache_keys,
    cache_values,
    new_counts,
    cached_lengths,
    deal,
):
    rows, width = tokens.shape
    requests = cache_keys.shape[0]
    new_slots = rows // requests
    model_width = attn_gain.shape[0]
    half = rows // 2
    params = pltpu.CompilerParams(vmem_limit_bytes=VMEM_LIMIT)
    x = lax.all_gather(tokens, ("hi", "lo"), axis=0, tiled=False)
    keep, send = pl.pallas_call(
        functools.partial(attend_kernel, replicas),
        out_shape=(
            jax.ShapeDtypeStruct((half, model_width), F32),
            jax.ShapeDtypeStruct((half, model_width), BF16),
        ),
        in_specs=[VMEM] * 6 + [SMEM] + [VMEM] * 2 + [SMEM] * 2 + [VMEM],
        out_specs=(VMEM, VMEM),
        compiler_params=params,
        name="attend",
    )(
        x,
        attn_gain.reshape(1, model_width),
        w_query,
        w_key,
        w_value,
        w_out,
        bias_table,
        cache_keys,
        cache_values,
        new_counts,
        cached_lengths,
        deal,
    )
    stream = pl.pallas_call(
        functools.partial(stream_kernel, replicas, new_slots),
        out_shape=jax.ShapeDtypeStruct((rows, model_width), BF16),
        in_specs=[VMEM, SMEM, VMEM],
        out_specs=VMEM,
        compiler_params=params,
        name="stream",
    )(x, new_counts, deal)
    pair = (keep + swap(send, "lo").astype(F32)).astype(BF16)
    total = (pair.astype(F32) + swap(pair, "hi").astype(F32)).astype(BF16)
    other = swap(total, "lo")
    groups = lax.axis_size("hi")
    keep, send = pl.pallas_call(
        ffn_kernel,
        out_shape=(
            jax.ShapeDtypeStruct((groups, rows, width), F32),
            jax.ShapeDtypeStruct((groups, rows, width), BF16),
        ),
        in_specs=[VMEM] * 6,
        out_specs=(VMEM, VMEM),
        compiler_params=params,
        name="ffn",
    )(total, other, stream, ffn_gain.reshape(1, model_width), w_inner, w_outer)
    pair = (keep + swap(send, "lo").astype(F32)).astype(BF16)
    parts = lax.all_to_all(
        pair.reshape(groups * replicas, rows // replicas, width), ("hi", "rep"), 0, 0, tiled=True
    )
    return jnp.sum(parts.reshape(groups, rows, width).astype(F32), axis=0).astype(BF16)


def solution(mesh):
    replicas, tp = mesh.shape["rep"], mesh.shape["tp"]
    split = Mesh(mesh.devices.reshape(replicas, tp // 2, 2), ("rep", "hi", "lo"))
    cols = ("hi", "lo")
    in_specs = (
        P("rep", cols),
        P(),
        P(),
        P(None, cols),
        P(None, cols),
        P(None, cols),
        P(cols, None),
        P(None, cols),
        P(cols, None),
        P(None, cols),
        P("rep", None, cols),
        P("rep", None, cols),
        P(None, "rep"),
        P(None, "rep"),
        P("rep", None),
    )
    return jax.shard_map(
        functools.partial(on_device, replicas),
        mesh=split,
        in_specs=in_specs,
        out_specs=P("rep", cols),
        check_vma=False,
    )
```

```python
import functools

import jax
import jax.numpy as jnp
from jax import lax
from jax.experimental import pallas as pl
from jax.experimental.pallas import tpu as pltpu
from jax.sharding import Mesh, PartitionSpec as P

EPSILON = 1e-06
THRESHOLDS = (1, 2, 3, 4, 5, 6, 7, 8, 12, 16, 23, 32, 46, 64, 91)
BF16 = jnp.bfloat16
F32 = jnp.float32
VMEM = pl.BlockSpec(memory_space=pltpu.VMEM)
SMEM = pl.BlockSpec(memory_space=pltpu.SMEM)
PREPARE_FLOPS = 7 * 10**9
VMEM_LIMIT = 24 * 1024 * 1024


def dot(a, b):
    return jnp.dot(a, b, preferred_element_type=F32)


def place():
    upper, lower = lax.axis_index("hi"), lax.axis_index("lo")
    return upper * 2 + lower, upper ^ lower


def deal_matrix(deal, counts_ref, replicas, new_slots, half, side):
    rows = deal.shape[1]
    share = rows // replicas
    lane = lax.broadcasted_iota(jnp.int32, (1, rows), 1)
    live = jnp.zeros((1, rows), jnp.bool_)
    for j in range(rows // new_slots):
        offset = lane - j * new_slots
        live = live | ((offset >= 0) & (offset < jnp.minimum(counts_ref[0, j], new_slots)))
    slot = lax.rem(deal, replicas) * share + lax.div(deal, replicas)
    slot = jnp.where(live, slot, -1)
    row = lax.broadcasted_iota(jnp.int32, (rows, rows), 0)
    row = jnp.where(side == 0, row, jnp.where(row < half, row + half, row - half))
    return jnp.where(row == slot, 1.0, 0.0).astype(BF16)


def bias_of(table_ref, relative, head):
    distance = jnp.abs(relative)
    before = jnp.full(relative.shape, table_ref[head, 0], F32)
    after = jnp.full(relative.shape, table_ref[head, 17], F32)
    for step, threshold in enumerate(THRESHOLDS):
        far = distance >= threshold
        before = jnp.where(far, table_ref[head, step + 1], before)
        after = jnp.where(far, table_ref[head, step + 17], after)
    return jnp.where(relative > 0, after, before)


def columns_of(index, xor, width):
    return pl.ds(pl.multiple_of((index ^ xor) * width, width), width)


def prepare_kernel(
    replicas,
    cached,
    new_slots,
    table_ref,
    counts_ref,
    lengths_ref,
    deal_ref,
    bias_ref,
    picked_ref,
):
    _, side = place()
    picked_ref[...] = deal_matrix(
        deal_ref[...], counts_ref, replicas, new_slots, picked_ref.shape[0] // 2, side
    )
    requests, _, key_slots = bias_ref.shape
    key_index = lax.broadcasted_iota(jnp.int32, (new_slots, key_slots), 1)
    query_index = lax.broadcasted_iota(jnp.int32, (new_slots, key_slots), 0)
    is_cache = key_index < cached
    for j in range(requests):
        length = lengths_ref[0, j]
        count = counts_ref[0, j]
        position = jnp.where(is_cache, key_index, length + key_index - cached)
        relative = position - (length + query_index)
        live = jnp.where(is_cache, key_index - length, key_index - cached - count) < 0
        for h in range(table_ref.shape[0]):
            bias = bias_of(table_ref, relative, h)
            bias_ref[j, h * new_slots : (h + 1) * new_slots] = jnp.where(live, bias, -1e30)


def attend_kernel(
    own_ref,
    far_ref,
    near_ref,
    near_far_ref,
    gain_ref,
    w_query_ref,
    w_key_ref,
    w_value_ref,
    w_out_ref,
    bias_ref,
    picked_ref,
    cache_keys_ref,
    cache_values_ref,
    keep_ref,
    send_ref,
):
    index, _ = place()
    rows, width = own_ref.shape
    model_width = gain_ref.shape[1]
    requests, cached, local_width = cache_keys_ref.shape
    new_slots = rows // requests
    head_count = bias_ref.shape[1] // new_slots
    head_size = local_width // head_count
    half = rows // 2

    blocks = [(own_ref[...], 0), (far_ref[...], 3), (near_ref[...], 1), (near_far_ref[...], 2)]
    squares = 0.0
    for block, _ in blocks:
        block = block.astype(F32)
        squares = squares + jnp.sum(block * block, axis=1, keepdims=True)
    inverse = lax.rsqrt(squares / model_width + EPSILON)
    queries = new_keys = new_values = 0.0
    for block, xor in blocks:
        columns = columns_of(index, xor, width)
        normed = (block.astype(F32) * inverse * gain_ref[:, columns]).astype(BF16)
        queries = queries + dot(normed, w_query_ref[columns, :])
        new_keys = new_keys + dot(normed, w_key_ref[columns, :])
        new_values = new_values + dot(normed, w_value_ref[columns, :])
    queries, new_keys, new_values = (v.astype(BF16) for v in (queries, new_keys, new_values))

    lane_head = lax.broadcasted_iota(jnp.int32, (new_slots, local_width), 1) // head_size
    contexts = []
    for j in range(requests):
        own = slice(j * new_slots, (j + 1) * new_slots)
        query = queries[own]
        stacked = jnp.concatenate(
            [jnp.where(lane_head == h, query, jnp.zeros_like(query)) for h in range(head_count)],
            axis=0,
        )
        keys = jnp.concatenate([cache_keys_ref[j], new_keys[own]], axis=0)
        values = jnp.concatenate([cache_values_ref[j], new_values[own]], axis=0)
        scores = lax.dot_general(
            stacked, keys, (((1,), (1,)), ((), ())), preferred_element_type=F32
        )
        scores = scores + bias_ref[j]
        weights = jnp.exp(scores - jnp.max(scores, axis=1, keepdims=True))
        probs = (weights / jnp.sum(weights, axis=1, keepdims=True)).astype(BF16)
        mixed = dot(probs, values)
        context = jnp.zeros((new_slots, local_width), F32)
        for h in range(head_count):
            context = jnp.where(lane_head == h, mixed[h * new_slots : (h + 1) * new_slots], context)
        contexts.append(context.astype(BF16))
    context = dot(picked_ref[...], jnp.concatenate(contexts, axis=0)).astype(BF16)
    send_ref[...] = dot(context[half:], w_out_ref[...]).astype(BF16)
    keep_ref[...] = dot(context[:half], w_out_ref[...])


def stream_kernel(own_ref, far_ref, near_ref, near_far_ref, picked_ref, stream_ref):
    index, _ = place()
    width = own_ref.shape[1]
    for ref, xor in ((own_ref, 0), (far_ref, 3), (near_ref, 1), (near_far_ref, 2)):
        stream_ref[:, columns_of(index, xor, width)] = dot(picked_ref[...], ref[...]).astype(BF16)


def ffn_kernel(own_ref, other_ref, stream_ref, gain_ref, w_inner_ref, w_outer_ref, keep_ref, send_ref):
    _, side = place()
    core = lax.axis_index("lo")
    upper = lax.axis_index("hi")
    half, model_width = own_ref.shape
    groups, _, width = keep_ref.shape
    for part, ref in enumerate((own_ref, other_ref)):
        start = pl.multiple_of((side ^ part) * half, half)
        mixed = ref[...].astype(F32) + stream_ref[part * half : (part + 1) * half].astype(F32)
        square = jnp.sum(mixed * mixed, axis=1, keepdims=True)
        inverse = lax.rsqrt(square / model_width + EPSILON)
        ffn_input = (mixed * inverse * gain_ref[...]).astype(BF16)
        hidden = jnp.maximum(dot(ffn_input, w_inner_ref[...]), 0.0).astype(BF16)
        projected = dot(hidden, w_outer_ref[...])
        for g in range(groups):
            for c in range(2):
                columns = slice((g * 2 + c) * width, (g * 2 + c + 1) * width)
                mine = (upper == g) & (core == c)
                value = projected[:, columns] + jnp.where(mine, mixed[:, columns], 0.0)

                @pl.when(core == c)
                def _():
                    keep_ref[g, pl.ds(start, half), :] = value

                @pl.when(core != c)
                def _():
                    send_ref[g, pl.ds(start, half), :] = value.astype(BF16)


def swap(value, xor):
    return lax.ppermute(value, ("hi", "lo"), [(i, i ^ xor) for i in range(4)])


def on_device(
    replicas,
    tokens,
    attn_gain,
    ffn_gain,
    w_query,
    w_key,
    w_value,
    w_out,
    w_inner,
    w_outer,
    bias_table,
    cache_keys,
    cache_values,
    new_counts,
    cached_lengths,
    deal,
):
    rows, width = tokens.shape
    requests = cache_keys.shape[0]
    new_slots = rows // requests
    model_width = attn_gain.shape[0]
    half = rows // 2
    params = pltpu.CompilerParams(vmem_limit_bytes=VMEM_LIMIT)
    far = swap(tokens, 3)
    near = swap(tokens, 1)
    cached, head_count = cache_keys.shape[1], bias_table.shape[1]
    shape = jax.ShapeDtypeStruct
    bias, picked = pl.pallas_call(
        functools.partial(prepare_kernel, replicas, cached, new_slots),
        out_shape=(
            shape((requests, head_count * new_slots, cached + new_slots), F32),
            shape((rows, rows), BF16),
        ),
        in_specs=[SMEM] * 3 + [VMEM],
        out_specs=(VMEM,) * 2,
        compiler_params=params,
        cost_estimate=pl.CostEstimate(flops=PREPARE_FLOPS, bytes_accessed=0, transcendentals=0),
        name="prepare",
    )(bias_table.T, new_counts.T, cached_lengths.T, deal)
    blocks = (tokens, far, near, swap(far, 1))
    keep, send = pl.pallas_call(
        attend_kernel,
        out_shape=(shape((half, model_width), F32), shape((half, model_width), BF16)),
        in_specs=[VMEM] * 13,
        out_specs=(VMEM, VMEM),
        compiler_params=params,
        name="attend",
    )(
        *blocks,
        attn_gain.reshape(1, model_width),
        w_query,
        w_key,
        w_value,
        w_out,
        bias,
        picked,
        cache_keys,
        cache_values,
    )
    stream = pl.pallas_call(
        stream_kernel,
        out_shape=shape((rows, model_width), BF16),
        in_specs=[VMEM] * 5,
        out_specs=VMEM,
        compiler_params=params,
        name="stream",
    )(*blocks, picked)
    pair = (keep + swap(send, 1).astype(F32)).astype(BF16)
    total = (pair.astype(F32) + swap(pair, 3).astype(F32)).astype(BF16)
    other = swap(total, 1)
    groups = lax.axis_size("hi")
    keep, send = pl.pallas_call(
        ffn_kernel,
        out_shape=(
            jax.ShapeDtypeStruct((groups, rows, width), F32),
            jax.ShapeDtypeStruct((groups, rows, width), BF16),
        ),
        in_specs=[VMEM] * 6,
        out_specs=(VMEM, VMEM),
        compiler_params=params,
        name="ffn",
    )(total, other, stream, ffn_gain.reshape(1, model_width), w_inner, w_outer)
    pair = (keep + swap(send, 1).astype(F32)).astype(BF16)
    parts = lax.all_to_all(
        pair.reshape(groups * replicas, rows // replicas, width), ("hi", "rep"), 0, 0, tiled=True
    )
    return jnp.sum(parts.reshape(groups, rows, width).astype(F32), axis=0).astype(BF16)


def solution(mesh):
    replicas, tp = mesh.shape["rep"], mesh.shape["tp"]
    split = Mesh(mesh.devices.reshape(replicas, tp // 2, 2), ("rep", "hi", "lo"))
    cols = ("hi", "lo")
    in_specs = (
        P("rep", cols),
        P(),
        P(),
        P(None, cols),
        P(None, cols),
        P(None, cols),
        P(cols, None),
        P(None, cols),
        P(cols, None),
        P(None, cols),
        P("rep", None, cols),
        P("rep", None, cols),
        P(None, "rep"),
        P(None, "rep"),
        P("rep", None),
    )
    return jax.shard_map(
        functools.partial(on_device, replicas),
        mesh=split,
        in_specs=in_specs,
        out_specs=P("rep", cols),
        check_vma=False,
    )
```

```python
import functools

import jax
import jax.numpy as jnp
from jax import lax
from jax.experimental import pallas as pl
from jax.experimental.pallas import tpu as pltpu
from jax.sharding import Mesh, PartitionSpec as P

EPSILON = 1e-06
THRESHOLDS = (1, 2, 3, 4, 5, 6, 7, 8, 12, 16, 23, 32, 46, 64, 91)
BF16 = jnp.bfloat16
F32 = jnp.float32
VMEM = pl.BlockSpec(memory_space=pltpu.VMEM)
SMEM = pl.BlockSpec(memory_space=pltpu.SMEM)
PREPARE_FLOPS = 7 * 10**9
VMEM_LIMIT = 24 * 1024 * 1024


def dot(a, b):
    return jnp.dot(a, b, preferred_element_type=F32)


def place():
    upper, lower = lax.axis_index("hi"), lax.axis_index("lo")
    return upper * 2 + lower, upper ^ lower


def deal_matrix(deal, counts_ref, replicas, new_slots, half, side):
    rows = deal.shape[1]
    share = rows // replicas
    lane = lax.broadcasted_iota(jnp.int32, (1, rows), 1)
    live = jnp.zeros((1, rows), jnp.bool_)
    for j in range(rows // new_slots):
        offset = lane - j * new_slots
        live = live | ((offset >= 0) & (offset < jnp.minimum(counts_ref[0, j], new_slots)))
    slot = lax.rem(deal, replicas) * share + lax.div(deal, replicas)
    slot = jnp.where(live, slot, -1)
    row = lax.broadcasted_iota(jnp.int32, (rows, rows), 0)
    row = jnp.where(side == 0, row, jnp.where(row < half, row + half, row - half))
    return jnp.where(row == slot, 1.0, 0.0).astype(BF16)


def bias_of(table_ref, relative, head):
    distance = jnp.abs(relative)
    before = jnp.full(relative.shape, table_ref[head, 0], F32)
    after = jnp.full(relative.shape, table_ref[head, 17], F32)
    for step, threshold in enumerate(THRESHOLDS):
        far = distance >= threshold
        before = jnp.where(far, table_ref[head, step + 1], before)
        after = jnp.where(far, table_ref[head, step + 17], after)
    return jnp.where(relative > 0, after, before)


def columns_of(index, xor, width):
    return pl.ds(pl.multiple_of((index ^ xor) * width, width), width)


def prepare_kernel(
    replicas,
    cached,
    new_slots,
    table_ref,
    counts_ref,
    lengths_ref,
    deal_ref,
    bias_ref,
    picked_ref,
):
    _, side = place()
    picked_ref[...] = deal_matrix(
        deal_ref[...], counts_ref, replicas, new_slots, picked_ref.shape[0] // 2, side
    )
    requests, _, key_slots = bias_ref.shape
    key_index = lax.broadcasted_iota(jnp.int32, (new_slots, key_slots), 1)
    query_index = lax.broadcasted_iota(jnp.int32, (new_slots, key_slots), 0)
    is_cache = key_index < cached
    for j in range(requests):
        length = lengths_ref[0, j]
        count = counts_ref[0, j]
        position = jnp.where(is_cache, key_index, length + key_index - cached)
        relative = position - (length + query_index)
        live = jnp.where(is_cache, key_index - length, key_index - cached - count) < 0
        for h in range(table_ref.shape[0]):
            bias = bias_of(table_ref, relative, h)
            bias_ref[j, h * new_slots : (h + 1) * new_slots] = jnp.where(live, bias, -1e30)


def attend_kernel(
    own_ref,
    far_ref,
    near_ref,
    near_far_ref,
    gain_ref,
    w_query_ref,
    w_key_ref,
    w_value_ref,
    w_out_ref,
    bias_ref,
    picked_ref,
    cache_keys_ref,
    cache_values_ref,
    send_ref,
    context_ref,
):
    index, _ = place()
    rows, width = own_ref.shape
    model_width = gain_ref.shape[1]
    requests, cached, local_width = cache_keys_ref.shape
    new_slots = rows // requests
    head_count = bias_ref.shape[1] // new_slots
    head_size = local_width // head_count
    half = rows // 2

    blocks = [(own_ref[...], 0), (far_ref[...], 3), (near_ref[...], 1), (near_far_ref[...], 2)]
    squares = 0.0
    for block, _ in blocks:
        block = block.astype(F32)
        squares = squares + jnp.sum(block * block, axis=1, keepdims=True)
    inverse = lax.rsqrt(squares / model_width + EPSILON)
    queries = new_keys = new_values = 0.0
    for block, xor in blocks:
        columns = columns_of(index, xor, width)
        normed = (block.astype(F32) * inverse * gain_ref[:, columns]).astype(BF16)
        queries = queries + dot(normed, w_query_ref[columns, :])
        new_keys = new_keys + dot(normed, w_key_ref[columns, :])
        new_values = new_values + dot(normed, w_value_ref[columns, :])
    queries, new_keys, new_values = (v.astype(BF16) for v in (queries, new_keys, new_values))

    lane_head = lax.broadcasted_iota(jnp.int32, (new_slots, local_width), 1) // head_size
    contexts = []
    for j in range(requests):
        own = slice(j * new_slots, (j + 1) * new_slots)
        query = queries[own]
        stacked = jnp.concatenate(
            [jnp.where(lane_head == h, query, jnp.zeros_like(query)) for h in range(head_count)],
            axis=0,
        )
        keys = jnp.concatenate([cache_keys_ref[j], new_keys[own]], axis=0)
        values = jnp.concatenate([cache_values_ref[j], new_values[own]], axis=0)
        scores = lax.dot_general(
            stacked, keys, (((1,), (1,)), ((), ())), preferred_element_type=F32
        )
        scores = scores + bias_ref[j]
        weights = jnp.exp(scores - jnp.max(scores, axis=1, keepdims=True))
        probs = (weights / jnp.sum(weights, axis=1, keepdims=True)).astype(BF16)
        mixed = dot(probs, values)
        context = jnp.zeros((new_slots, local_width), F32)
        for h in range(head_count):
            context = jnp.where(lane_head == h, mixed[h * new_slots : (h + 1) * new_slots], context)
        contexts.append(context.astype(BF16))
    context = dot(picked_ref[...], jnp.concatenate(contexts, axis=0)).astype(BF16)
    send_ref[...] = dot(context[half:], w_out_ref[...]).astype(BF16)
    context_ref[...] = context[:half]


def project_kernel(context_ref, w_out_ref, keep_ref):
    keep_ref[...] = dot(context_ref[...], w_out_ref[...])


def stream_kernel(own_ref, far_ref, near_ref, near_far_ref, picked_ref, stream_ref):
    index, _ = place()
    width = own_ref.shape[1]
    for ref, xor in ((own_ref, 0), (far_ref, 3), (near_ref, 1), (near_far_ref, 2)):
        stream_ref[:, columns_of(index, xor, width)] = dot(picked_ref[...], ref[...]).astype(BF16)


def hidden_of(total_ref, stream_ref, gain_ref, w_inner_ref):
    mixed = total_ref[...].astype(F32) + stream_ref[...].astype(F32)
    square = jnp.sum(mixed * mixed, axis=1, keepdims=True)
    inverse = lax.rsqrt(square / mixed.shape[1] + EPSILON)
    ffn_input = (mixed * inverse * gain_ref[...]).astype(BF16)
    return jnp.maximum(dot(ffn_input, w_inner_ref[...]), 0.0).astype(BF16)


def inner_kernel(total_ref, stream_ref, gain_ref, w_inner_ref, hidden_ref):
    hidden_ref[...] = hidden_of(total_ref, stream_ref.at[: total_ref.shape[0]], gain_ref, w_inner_ref)


def send_kernel(
    total_ref, stream_ref, gain_ref, w_inner_ref, w_outer_ref, first_ref, second_ref, send_ref
):
    core = lax.axis_index("lo")
    _, side = place()
    half = total_ref.shape[0]
    groups, _, width = send_ref.shape
    second = hidden_of(total_ref, stream_ref.at[half:], gain_ref, w_inner_ref)
    second_ref[...] = second
    for g in range(groups):
        weight = w_outer_ref[:, columns_of(g * 2 + 1 - core, 0, width)]
        for part, hidden in enumerate((first_ref[...], second)):
            start = pl.multiple_of((side ^ part) * half, half)
            send_ref[g, pl.ds(start, half), :] = dot(hidden, weight).astype(BF16)


def keep_kernel(own_ref, other_ref, stream_ref, first_ref, second_ref, w_outer_ref, keep_ref):
    core, upper = lax.axis_index("lo"), lax.axis_index("hi")
    index, side = place()
    half = own_ref.shape[0]
    groups, _, width = keep_ref.shape
    columns = columns_of(index, 0, width)
    for part, total_ref, hidden_ref in ((0, own_ref, first_ref), (1, other_ref, second_ref)):
        start = pl.multiple_of((side ^ part) * half, half)
        rows = slice(part * half, (part + 1) * half)
        mixed = total_ref[:, columns].astype(F32) + stream_ref[rows, columns].astype(F32)
        for g in range(groups):
            weight = w_outer_ref[:, columns_of(g * 2 + core, 0, width)]
            value = dot(hidden_ref[...], weight) + jnp.where(upper == g, mixed, 0.0)
            keep_ref[g, pl.ds(start, half), :] = value


def swap(value, xor):
    return lax.ppermute(value, ("hi", "lo"), [(i, i ^ xor) for i in range(4)])


def on_device(
    replicas,
    tokens,
    attn_gain,
    ffn_gain,
    w_query,
    w_key,
    w_value,
    w_out,
    w_inner,
    w_outer,
    bias_table,
    cache_keys,
    cache_values,
    new_counts,
    cached_lengths,
    deal,
):
    rows, width = tokens.shape
    requests = cache_keys.shape[0]
    new_slots = rows // requests
    model_width = attn_gain.shape[0]
    half = rows // 2
    params = pltpu.CompilerParams(vmem_limit_bytes=VMEM_LIMIT)
    far = swap(tokens, 3)
    cached, head_count = cache_keys.shape[1], bias_table.shape[1]
    shape = jax.ShapeDtypeStruct
    bias, picked = pl.pallas_call(
        functools.partial(prepare_kernel, replicas, cached, new_slots),
        out_shape=(
            shape((requests, head_count * new_slots, cached + new_slots), F32),
            shape((rows, rows), BF16),
        ),
        in_specs=[SMEM] * 3 + [VMEM],
        out_specs=(VMEM,) * 2,
        compiler_params=params,
        cost_estimate=pl.CostEstimate(flops=PREPARE_FLOPS, bytes_accessed=0, transcendentals=0),
        name="prepare",
    )(bias_table.T, new_counts.T, cached_lengths.T, deal)
    far, own, bias, picked = lax.optimization_barrier((far, tokens, bias, picked))
    blocks = (tokens, far, swap(own, 1), swap(far, 1))
    send, context = pl.pallas_call(
        attend_kernel,
        out_shape=(shape((half, model_width), BF16), shape((half, w_out.shape[0]), BF16)),
        in_specs=[VMEM] * 13,
        out_specs=(VMEM, VMEM),
        compiler_params=params,
        name="attend",
    )(
        *blocks,
        attn_gain.reshape(1, model_width),
        w_query,
        w_key,
        w_value,
        w_out,
        bias,
        picked,
        cache_keys,
        cache_values,
    )
    local = functools.partial(pl.pallas_call, compiler_params=params)
    keep = local(
        project_kernel,
        out_shape=shape((half, model_width), F32),
        in_specs=[VMEM] * 2,
        out_specs=VMEM,
        name="project",
    )(context, w_out)
    stream = local(
        stream_kernel,
        out_shape=shape((rows, model_width), BF16),
        in_specs=[VMEM] * 5,
        out_specs=VMEM,
        name="stream",
    )(*blocks, picked)
    pair = (keep + swap(send, 1).astype(F32)).astype(BF16)
    total = (pair.astype(F32) + swap(pair, 3).astype(F32)).astype(BF16)
    other = swap(total, 1)
    gain = ffn_gain.reshape(1, model_width)
    hidden_shape = shape((half, w_inner.shape[1]), BF16)
    first = local(
        inner_kernel,
        out_shape=hidden_shape,
        in_specs=[VMEM] * 4,
        out_specs=VMEM,
        name="inner",
    )(total, stream, gain, w_inner)
    groups = lax.axis_size("hi")
    second, send = local(
        send_kernel,
        out_shape=(hidden_shape, shape((groups, rows, width), BF16)),
        in_specs=[VMEM] * 6,
        out_specs=(VMEM, VMEM),
        name="send",
    )(other, stream, gain, w_inner, w_outer, first)
    keep = local(
        keep_kernel,
        out_shape=shape((groups, rows, width), F32),
        in_specs=[VMEM] * 6,
        out_specs=VMEM,
        name="keep",
    )(total, other, stream, first, second, w_outer)
    pair = (keep + swap(send, 1).astype(F32)).astype(BF16)
    parts = lax.all_to_all(
        pair.reshape(groups * replicas, rows // replicas, width), ("hi", "rep"), 0, 0, tiled=True
    )
    return jnp.sum(parts.reshape(groups, rows, width).astype(F32), axis=0).astype(BF16)


def solution(mesh):
    replicas, tp = mesh.shape["rep"], mesh.shape["tp"]
    split = Mesh(mesh.devices.reshape(replicas, tp // 2, 2), ("rep", "hi", "lo"))
    cols = ("hi", "lo")
    in_specs = (
        P("rep", cols),
        P(),
        P(),
        P(None, cols),
        P(None, cols),
        P(None, cols),
        P(cols, None),
        P(None, cols),
        P(cols, None),
        P(None, cols),
        P("rep", None, cols),
        P("rep", None, cols),
        P(None, "rep"),
        P(None, "rep"),
        P("rep", None),
    )
    return jax.shard_map(
        functools.partial(on_device, replicas),
        mesh=split,
        in_specs=in_specs,
        out_specs=P("rep", cols),
        check_vma=False,
    )
```

```python
import functools

import jax
import jax.numpy as jnp
from jax import lax
from jax.experimental import pallas as pl
from jax.experimental.pallas import tpu as pltpu
from jax.sharding import Mesh, PartitionSpec as P

EPSILON = 1e-06
THRESHOLDS = (1, 2, 3, 4, 5, 6, 7, 8, 12, 16, 23, 32, 46, 64, 91)
BF16 = jnp.bfloat16
F32 = jnp.float32
VMEM = pl.BlockSpec(memory_space=pltpu.VMEM)
SMEM = pl.BlockSpec(memory_space=pltpu.SMEM)
PREPARE_FLOPS = 7 * 10**9
INNER_FLOPS = 40 * 10**9
VMEM_LIMIT = 24 * 1024 * 1024


def dot(a, b):
    return jnp.dot(a, b, preferred_element_type=F32)


def place():
    upper, lower = lax.axis_index("hi"), lax.axis_index("lo")
    return upper * 2 + lower, upper ^ lower


def columns_of(index, width):
    return pl.ds(pl.multiple_of(index * width, width), width)


def bias_of(table_ref, relative, head):
    distance = jnp.abs(relative)
    before = jnp.full(relative.shape, table_ref[head, 0], F32)
    after = jnp.full(relative.shape, table_ref[head, 17], F32)
    for step, threshold in enumerate(THRESHOLDS):
        far = distance >= threshold
        before = jnp.where(far, table_ref[head, step + 1], before)
        after = jnp.where(far, table_ref[head, step + 17], after)
    return jnp.where(relative > 0, after, before)


def prepare_kernel(
    replicas, cached, table_ref, counts_ref, lengths_ref, deal_ref, bias_ref, picked_ref
):
    _, side = place()
    rows = deal_ref.shape[1]
    new_slots = rows // 2
    deal = deal_ref[...]
    slot = lax.rem(deal, replicas) * (rows // replicas) + lax.div(deal, replicas)
    lane = lax.broadcasted_iota(jnp.int32, (1, rows), 1)
    live = lane < jnp.where(
        lane < new_slots, counts_ref[0, 0], jnp.minimum(counts_ref[0, 1], new_slots) + new_slots
    )
    slot = jnp.where(live, slot, -1)
    turned = jnp.concatenate([slot[:, new_slots:], slot[:, :new_slots]], axis=1)
    slot = jnp.where(side == 0, slot, turned)[:, :new_slots]
    row = lax.broadcasted_iota(jnp.int32, (rows, new_slots), 0)
    picked_ref[...] = jnp.where(row == slot, 1.0, 0.0).astype(BF16)

    requests, _, key_slots = bias_ref.shape
    key_index = lax.broadcasted_iota(jnp.int32, (new_slots, key_slots), 1)
    query_index = lax.broadcasted_iota(jnp.int32, (new_slots, key_slots), 0)
    is_cache = key_index < cached
    for j in range(requests):
        length, count = lengths_ref[0, j], counts_ref[0, j]
        position = jnp.where(is_cache, key_index, length + key_index - cached)
        relative = position - (length + query_index)
        live = jnp.where(is_cache, key_index - length, key_index - cached - count) < 0
        for h in range(table_ref.shape[0]):
            bias = jnp.where(live, bias_of(table_ref, relative, h), -1e30)
            bias_ref[j, h * new_slots : (h + 1) * new_slots] = bias


def attend(query, new_keys, new_values, old_keys, old_values, bias):
    new_slots, local_width = query.shape
    head_count = bias.shape[0] // new_slots
    lane = lax.broadcasted_iota(jnp.int32, (new_slots, local_width), 1)
    lane_head = lane // (local_width // head_count)
    stacked = jnp.concatenate(
        [jnp.where(lane_head == h, query, jnp.zeros_like(query)) for h in range(head_count)],
        axis=0,
    )
    keys = jnp.concatenate([old_keys, new_keys], axis=0)
    values = jnp.concatenate([old_values, new_values], axis=0)
    scores = lax.dot_general(stacked, keys, (((1,), (1,)), ((), ())), preferred_element_type=F32)
    scores = scores + bias
    weights = jnp.exp(scores - jnp.max(scores, axis=1, keepdims=True))
    probs = (weights / jnp.sum(weights, axis=1, keepdims=True)).astype(BF16)
    mixed = dot(probs, values)
    context = jnp.zeros((new_slots, local_width), F32)
    for h in range(head_count):
        context = jnp.where(lane_head == h, mixed[h * new_slots : (h + 1) * new_slots], context)
    return context.astype(BF16)


def first_kernel(
    own_ref,
    near_ref,
    far_ref,
    across_ref,
    gain_ref,
    w_query_ref,
    w_key_ref,
    w_value_ref,
    w_out_ref,
    cache_keys_ref,
    cache_values_ref,
    bias_ref,
    send_ref,
    query_ref,
    key_ref,
    value_ref,
):
    index, side = place()
    rows, width = own_ref.shape
    model_width = gain_ref.shape[1]
    new_slots = rows // 2
    blocks = [(own_ref, 0), (near_ref, 1), (far_ref, 3), (across_ref, 2)]
    squares = 0.0
    for ref, _ in blocks:
        block = ref[...].astype(F32)
        squares = squares + jnp.sum(block * block, axis=1, keepdims=True)
    inverse = lax.rsqrt(squares / model_width + EPSILON)
    queries = new_keys = new_values = 0.0
    for ref, xor in blocks:
        columns = columns_of(index ^ xor, width)
        normed = (ref[...].astype(F32) * inverse * gain_ref[:, columns]).astype(BF16)
        queries = queries + dot(normed, w_query_ref[columns, :])
        new_keys = new_keys + dot(normed, w_key_ref[columns, :])
        new_values = new_values + dot(normed, w_value_ref[columns, :])
    query_ref[...] = queries.astype(BF16)
    key_ref[...] = new_keys.astype(BF16)
    value_ref[...] = new_values.astype(BF16)
    other = 1 - side
    own = columns_of(other, new_slots)
    context = attend(
        query_ref[own, :],
        key_ref[own, :],
        value_ref[own, :],
        cache_keys_ref[other],
        cache_values_ref[other],
        bias_ref[other],
    )
    send_ref[...] = dot(context, w_out_ref[...]).astype(BF16)


def second_kernel(
    query_ref, key_ref, value_ref, w_out_ref, cache_keys_ref, cache_values_ref, bias_ref, keep_ref
):
    _, side = place()
    own = columns_of(side, keep_ref.shape[0])
    context = attend(
        query_ref[own, :],
        key_ref[own, :],
        value_ref[own, :],
        cache_keys_ref[side],
        cache_values_ref[side],
        bias_ref[side],
    )
    keep_ref[...] = dot(context, w_out_ref[...])


def stream_kernel(own_ref, near_ref, far_ref, across_ref, stream_ref):
    index, side = place()
    width = own_ref.shape[1]
    rows = columns_of(side, stream_ref.shape[0])
    for ref, xor in ((own_ref, 0), (near_ref, 1), (far_ref, 3), (across_ref, 2)):
        stream_ref[:, columns_of(index ^ xor, width)] = ref[rows, :]


def project(hidden_refs, w_outer_refs, mixed_ref, picked_ref, group, core):
    upper = lax.axis_index("hi")
    width = mixed_ref.shape[1] // 4
    columns = columns_of(group * 2 + core, width)
    value = jnp.where(upper == group, mixed_ref[:, columns], 0.0)
    for hidden_ref, w_outer_ref in zip(hidden_refs, w_outer_refs):
        value = value + dot(hidden_ref[...], w_outer_ref[:, columns])
    return dot(picked_ref[...], value.astype(BF16)).astype(BF16)


def inner_kernel(
    pair_ref, other_ref, stream_ref, gain_ref, w_inner_ref, mixed_ref, input_ref, hidden_ref
):
    mixed = pair_ref[...].astype(F32) + other_ref[...].astype(F32) + stream_ref[...].astype(F32)
    mixed_ref[...] = mixed
    square = jnp.sum(mixed * mixed, axis=1, keepdims=True)
    inverse = lax.rsqrt(square / mixed.shape[1] + EPSILON)
    ffn_input = (mixed * inverse * gain_ref[...]).astype(BF16)
    input_ref[...] = ffn_input
    hidden_ref[...] = jnp.maximum(dot(ffn_input, w_inner_ref[...]), 0.0).astype(BF16)


def send_kernel(
    mixed_ref,
    input_ref,
    own_hidden_ref,
    near_inner_ref,
    own_outer_ref,
    near_outer_ref,
    picked_ref,
    near_hidden_ref,
    send_ref,
):
    hidden = jnp.maximum(dot(input_ref[...], near_inner_ref[...]), 0.0)
    near_hidden_ref[...] = hidden.astype(BF16)
    hidden_refs, outer_refs = (own_hidden_ref, near_hidden_ref), (own_outer_ref, near_outer_ref)
    core = 1 - lax.axis_index("lo")
    for g in range(send_ref.shape[0]):
        send_ref[g] = project(hidden_refs, outer_refs, mixed_ref, picked_ref, g, core)


def keep_kernel(
    mixed_ref,
    own_hidden_ref,
    near_hidden_ref,
    own_outer_ref,
    near_outer_ref,
    picked_ref,
    keep_ref,
):
    hidden_refs, outer_refs = (own_hidden_ref, near_hidden_ref), (own_outer_ref, near_outer_ref)
    core = lax.axis_index("lo")
    for g in range(keep_ref.shape[0]):
        keep_ref[g] = project(hidden_refs, outer_refs, mixed_ref, picked_ref, g, core)


def swap(value, xor):
    return lax.ppermute(value, ("hi", "lo"), [(i, i ^ xor) for i in range(4)])


def on_device(
    replicas,
    tokens,
    attn_gain,
    ffn_gain,
    w_query,
    w_key,
    w_value,
    w_out,
    w_inner,
    w_outer,
    bias_table,
    cache_keys,
    cache_values,
    new_counts,
    cached_lengths,
    deal,
):
    rows, width = tokens.shape
    requests, cached, local_width = cache_keys.shape
    new_slots = rows // requests
    model_width = attn_gain.shape[0]
    head_count = bias_table.shape[1]
    groups = lax.axis_size("hi")
    shape = jax.ShapeDtypeStruct
    local = functools.partial(
        pl.pallas_call, compiler_params=pltpu.CompilerParams(vmem_limit_bytes=VMEM_LIMIT)
    )
    across, far = swap(tokens, 2), swap(tokens, 3)
    bias, picked = local(
        functools.partial(prepare_kernel, replicas, cached),
        out_shape=(
            shape((requests, head_count * new_slots, cached + new_slots), F32),
            shape((rows, new_slots), BF16),
        ),
        in_specs=[SMEM] * 3 + [VMEM],
        out_specs=(VMEM,) * 2,
        cost_estimate=pl.CostEstimate(flops=PREPARE_FLOPS, bytes_accessed=0, transcendentals=0),
        name="prepare",
    )(bias_table.T, new_counts.T, cached_lengths.T, deal)
    late, bias, picked = lax.optimization_barrier((tokens, bias, picked))
    blocks = (tokens, swap(late, 1), far, across)
    projected = shape((rows, local_width), BF16)
    send, *projections = local(
        first_kernel,
        out_shape=(shape((new_slots, model_width), BF16),) + (projected,) * 3,
        in_specs=[VMEM] * 12,
        out_specs=(VMEM,) * 4,
        name="first",
    )(
        *blocks,
        attn_gain.reshape(1, model_width),
        w_query,
        w_key,
        w_value,
        w_out,
        cache_keys,
        cache_values,
        bias,
    )
    keep = local(
        second_kernel,
        out_shape=shape((new_slots, model_width), F32),
        in_specs=[VMEM] * 7,
        out_specs=VMEM,
        name="second",
    )(*projections, w_out, cache_keys, cache_values, bias)
    stream = local(
        stream_kernel,
        out_shape=shape((new_slots, model_width), BF16),
        in_specs=[VMEM] * 4,
        out_specs=VMEM,
        name="stream",
    )(*blocks)
    pair = (keep + swap(send, 1).astype(F32)).astype(BF16)
    late_inner, late_outer, pair = lax.optimization_barrier((w_inner, w_outer, pair))
    ff_width = w_inner.shape[1]
    hidden = shape((new_slots, ff_width), BF16)
    dealt = shape((groups, rows, width), BF16)
    mixed, ffn_input, first = local(
        inner_kernel,
        out_shape=(
            shape((new_slots, model_width), F32),
            shape((new_slots, model_width), BF16),
            hidden,
        ),
        in_specs=[VMEM] * 5,
        out_specs=(VMEM,) * 3,
        cost_estimate=pl.CostEstimate(flops=INNER_FLOPS, bytes_accessed=0, transcendentals=0),
        name="inner",
    )(pair, swap(pair, 3), stream, ffn_gain.reshape(1, model_width), w_inner)
    outer = (w_outer, swap(late_outer, 1))
    second, send = local(
        send_kernel,
        out_shape=(hidden, dealt),
        in_specs=[VMEM] * 7,
        out_specs=(VMEM,) * 2,
        name="send",
    )(mixed, ffn_input, first, swap(late_inner, 1), *outer, picked)
    keep = local(
        keep_kernel,
        out_shape=dealt,
        in_specs=[VMEM] * 6,
        out_specs=VMEM,
        name="keep",
    )(mixed, first, second, *outer, picked)
    pair = keep + swap(send, 1)
    parts = lax.all_to_all(
        pair.reshape(groups * replicas, rows // replicas, width), ("hi", "rep"), 0, 0, tiled=True
    )
    return jnp.sum(parts.reshape(groups, rows, width).astype(F32), axis=0).astype(BF16)


def solution(mesh):
    replicas, tp = mesh.shape["rep"], mesh.shape["tp"]
    split = Mesh(mesh.devices.reshape(replicas, tp // 2, 2), ("rep", "hi", "lo"))
    cols = ("hi", "lo")
    in_specs = (
        P("rep", cols),
        P(),
        P(),
        P(None, cols),
        P(None, cols),
        P(None, cols),
        P(cols, None),
        P(None, cols),
        P(cols, None),
        P(None, cols),
        P("rep", None, cols),
        P("rep", None, cols),
        P(None, "rep"),
        P(None, "rep"),
        P("rep", None),
    )
    return jax.shard_map(
        functools.partial(on_device, replicas),
        mesh=split,
        in_specs=in_specs,
        out_specs=P("rep", cols),
        check_vma=False,
    )
```

```python
import functools

import jax
import jax.numpy as jnp
from jax import lax
from jax.experimental import pallas as pl
from jax.experimental.pallas import tpu as pltpu
from jax.sharding import Mesh, PartitionSpec as P

EPSILON = 1e-06
THRESHOLDS = (1, 2, 3, 4, 5, 6, 7, 8, 12, 16, 23, 32, 46, 64, 91)
BF16 = jnp.bfloat16
F32 = jnp.float32
VMEM = pl.BlockSpec(memory_space=pltpu.VMEM)
SMEM = pl.BlockSpec(memory_space=pltpu.SMEM)
PREPARE_FLOPS = 7 * 10**9
INNER_FLOPS = 40 * 10**9
VMEM_LIMIT = 24 * 1024 * 1024


def dot(a, b):
    return jnp.dot(a, b, preferred_element_type=F32)


def place():
    upper, lower = lax.axis_index("hi"), lax.axis_index("lo")
    return upper * 2 + lower, lower


def halved(share):
    return share % 2 == 0


def columns_of(index, width):
    return pl.ds(pl.multiple_of(index * width, width), width)


def bias_of(table_ref, relative, head):
    distance = jnp.abs(relative)
    before = jnp.full(relative.shape, table_ref[head, 0], F32)
    after = jnp.full(relative.shape, table_ref[head, 17], F32)
    for step, threshold in enumerate(THRESHOLDS):
        far = distance >= threshold
        before = jnp.where(far, table_ref[head, step + 1], before)
        after = jnp.where(far, table_ref[head, step + 17], after)
    return jnp.where(relative > 0, after, before)


def prepare_kernel(
    replicas, cached, table_ref, counts_ref, lengths_ref, deal_ref, bias_ref, picked_ref
):
    _, side = place()
    rows = deal_ref.shape[1]
    new_slots = rows // 2
    half, share = rows // 2, rows // replicas
    deal = deal_ref[...]
    slot = lax.rem(deal, replicas) * share + lax.div(deal, replicas)
    lane = lax.broadcasted_iota(jnp.int32, (1, rows), 1)
    live = lane < jnp.where(
        lane < new_slots, counts_ref[0, 0], jnp.minimum(counts_ref[0, 1], new_slots) + new_slots
    )
    slot = jnp.where(live, slot, -1)
    row = lax.broadcasted_iota(jnp.int32, (rows, rows), 0)
    part = jnp.where(row < half, side, 1 - side)
    row = jnp.where(row < half, row, row - half)
    if halved(share):
        row = lax.div(row, share // 2) * share + part * (share // 2) + lax.rem(row, share // 2)
    else:
        row = part * half + row
    picked_ref[...] = jnp.where(row == slot, 1.0, 0.0).astype(BF16)

    requests, _, key_slots = bias_ref.shape
    key_index = lax.broadcasted_iota(jnp.int32, (new_slots, key_slots), 1)
    query_index = lax.broadcasted_iota(jnp.int32, (new_slots, key_slots), 0)
    is_cache = key_index < cached
    for j in range(requests):
        length, count = lengths_ref[0, j], counts_ref[0, j]
        position = jnp.where(is_cache, key_index, length + key_index - cached)
        relative = position - (length + query_index)
        live = jnp.where(is_cache, key_index - length, key_index - cached - count) < 0
        for h in range(table_ref.shape[0]):
            bias = jnp.where(live, bias_of(table_ref, relative, h), -1e30)
            bias_ref[j, h * new_slots : (h + 1) * new_slots] = bias


def attend(query, new_keys, new_values, old_keys, old_values, bias):
    new_slots, local_width = query.shape
    head_count = bias.shape[0] // new_slots
    lane = lax.broadcasted_iota(jnp.int32, (new_slots, local_width), 1)
    lane_head = lane // (local_width // head_count)
    stacked = jnp.concatenate(
        [jnp.where(lane_head == h, query, jnp.zeros_like(query)) for h in range(head_count)],
        axis=0,
    )
    keys = jnp.concatenate([old_keys, new_keys], axis=0)
    values = jnp.concatenate([old_values, new_values], axis=0)
    scores = lax.dot_general(stacked, keys, (((1,), (1,)), ((), ())), preferred_element_type=F32)
    scores = scores + bias
    weights = jnp.exp(scores - jnp.max(scores, axis=1, keepdims=True))
    probs = (weights / jnp.sum(weights, axis=1, keepdims=True)).astype(BF16)
    mixed = dot(probs, values)
    context = jnp.zeros((new_slots, local_width), F32)
    for h in range(head_count):
        context = jnp.where(lane_head == h, mixed[h * new_slots : (h + 1) * new_slots], context)
    return context.astype(BF16)


def attend_kernel(
    own_ref,
    near_ref,
    far_ref,
    across_ref,
    gain_ref,
    w_query_ref,
    w_key_ref,
    w_value_ref,
    w_out_ref,
    cache_keys_ref,
    cache_values_ref,
    bias_ref,
    picked_ref,
    send_ref,
    context_ref,
):
    index, _ = place()
    rows, width = own_ref.shape
    model_width = gain_ref.shape[1]
    requests = bias_ref.shape[0]
    new_slots, half = rows // requests, rows // 2
    blocks = [(own_ref, 0), (near_ref, 1), (far_ref, 3), (across_ref, 2)]
    squares = 0.0
    for ref, _ in blocks:
        block = ref[...].astype(F32)
        squares = squares + jnp.sum(block * block, axis=1, keepdims=True)
    inverse = lax.rsqrt(squares / model_width + EPSILON)
    queries = new_keys = new_values = 0.0
    for ref, xor in blocks:
        columns = columns_of(index ^ xor, width)
        normed = (ref[...].astype(F32) * inverse * gain_ref[:, columns]).astype(BF16)
        queries = queries + dot(normed, w_query_ref[columns, :])
        new_keys = new_keys + dot(normed, w_key_ref[columns, :])
        new_values = new_values + dot(normed, w_value_ref[columns, :])
    queries, new_keys, new_values = (v.astype(BF16) for v in (queries, new_keys, new_values))
    contexts = []
    for j in range(requests):
        own = slice(j * new_slots, (j + 1) * new_slots)
        contexts.append(
            attend(
                queries[own],
                new_keys[own],
                new_values[own],
                cache_keys_ref[j],
                cache_values_ref[j],
                bias_ref[j],
            )
        )
    context = dot(picked_ref[...], jnp.concatenate(contexts, axis=0)).astype(BF16)
    send_ref[...] = dot(context[half:], w_out_ref[...]).astype(BF16)
    context_ref[...] = context[:half]


def project_kernel(context_ref, w_out_ref, keep_ref):
    keep_ref[...] = dot(context_ref[...], w_out_ref[...])


def stream_kernel(own_ref, near_ref, far_ref, across_ref, picked_ref, stream_ref):
    index, _ = place()
    width = own_ref.shape[1]
    picked = picked_ref[: stream_ref.shape[0]]
    for ref, xor in ((own_ref, 0), (near_ref, 1), (far_ref, 3), (across_ref, 2)):
        stream_ref[:, columns_of(index ^ xor, width)] = dot(picked, ref[...]).astype(BF16)


def inner_kernel(
    pair_ref, other_ref, stream_ref, gain_ref, w_inner_ref, mixed_ref, input_ref, hidden_ref
):
    mixed = pair_ref[...].astype(F32) + other_ref[...].astype(F32) + stream_ref[...].astype(F32)
    mixed_ref[...] = mixed
    square = jnp.sum(mixed * mixed, axis=1, keepdims=True)
    inverse = lax.rsqrt(square / mixed.shape[1] + EPSILON)
    ffn_input = (mixed * inverse * gain_ref[...]).astype(BF16)
    input_ref[...] = ffn_input
    hidden_ref[...] = jnp.maximum(dot(ffn_input, w_inner_ref[...]), 0.0).astype(BF16)


def outer_kernel(
    mixed_ref,
    input_ref,
    own_hidden_ref,
    near_inner_ref,
    own_outer_ref,
    near_outer_ref,
    out_ref,
):
    upper = lax.axis_index("hi")
    width = out_ref.shape[2]
    hidden = jnp.maximum(dot(input_ref[...], near_inner_ref[...]), 0.0).astype(BF16)
    for t in range(out_ref.shape[0]):
        columns = slice(t * width, (t + 1) * width)
        value = dot(own_hidden_ref[...], own_outer_ref[:, columns])
        value = value + dot(hidden, near_outer_ref[:, columns])
        value = value + jnp.where(upper == t // 2, mixed_ref[:, columns], 0.0)
        out_ref[t] = value.astype(BF16)


def swap(value, xor):
    return lax.ppermute(value, ("hi", "lo"), [(i, i ^ xor) for i in range(4)])


def on_device(
    replicas,
    tokens,
    attn_gain,
    ffn_gain,
    w_query,
    w_key,
    w_value,
    w_out,
    w_inner,
    w_outer,
    bias_table,
    cache_keys,
    cache_values,
    new_counts,
    cached_lengths,
    deal,
):
    rows, width = tokens.shape
    requests, cached, local_width = cache_keys.shape
    new_slots = rows // requests
    model_width = attn_gain.shape[0]
    head_count = bias_table.shape[1]
    groups = lax.axis_size("hi")
    _, side = place()
    shape = jax.ShapeDtypeStruct
    local = functools.partial(
        pl.pallas_call, compiler_params=pltpu.CompilerParams(vmem_limit_bytes=VMEM_LIMIT)
    )
    across, far = swap(tokens, 2), swap(tokens, 3)
    bias, picked = local(
        functools.partial(prepare_kernel, replicas, cached),
        out_shape=(
            shape((requests, head_count * new_slots, cached + new_slots), F32),
            shape((rows, rows), BF16),
        ),
        in_specs=[SMEM] * 3 + [VMEM],
        out_specs=(VMEM,) * 2,
        cost_estimate=pl.CostEstimate(flops=PREPARE_FLOPS, bytes_accessed=0, transcendentals=0),
        name="prepare",
    )(bias_table.T, new_counts.T, cached_lengths.T, deal)
    late, bias, picked = lax.optimization_barrier((tokens, bias, picked))
    blocks = (tokens, swap(late, 1), far, across)
    half = rows // 2
    send, context = local(
        attend_kernel,
        out_shape=(shape((half, model_width), BF16), shape((half, local_width), BF16)),
        in_specs=[VMEM] * 13,
        out_specs=(VMEM,) * 2,
        name="attend",
    )(
        *blocks,
        attn_gain.reshape(1, model_width),
        w_query,
        w_key,
        w_value,
        w_out,
        cache_keys,
        cache_values,
        bias,
        picked,
    )
    keep = local(
        project_kernel,
        out_shape=shape((half, model_width), F32),
        in_specs=[VMEM] * 2,
        out_specs=VMEM,
        name="project",
    )(context, w_out)
    stream = local(
        stream_kernel,
        out_shape=shape((half, model_width), BF16),
        in_specs=[VMEM] * 5,
        out_specs=VMEM,
        name="stream",
    )(*blocks, picked)
    pair = (keep + swap(send, 1).astype(F32)).astype(BF16)
    late_inner, late_outer, pair = lax.optimization_barrier((w_inner, w_outer, pair))
    ff_width = w_inner.shape[1]
    mixed, ffn_input, hidden = local(
        inner_kernel,
        out_shape=(
            shape((half, model_width), F32),
            shape((half, model_width), BF16),
            shape((half, ff_width), BF16),
        ),
        in_specs=[VMEM] * 5,
        out_specs=(VMEM,) * 3,
        cost_estimate=pl.CostEstimate(flops=INNER_FLOPS, bytes_accessed=0, transcendentals=0),
        name="inner",
    )(pair, swap(pair, 2), stream, ffn_gain.reshape(1, model_width), w_inner)
    out = local(
        outer_kernel,
        out_shape=shape((groups * 2, half, width), BF16),
        in_specs=[VMEM] * 6,
        out_specs=VMEM,
        name="outer",
    )(mixed, ffn_input, hidden, swap(late_inner, 1), w_outer, swap(late_outer, 1))
    share = rows // replicas
    if not halved(share):
        padded = jnp.zeros((groups * 2, rows, width), BF16)
        out = lax.dynamic_update_slice_in_dim(padded, out, side * half, 1)
    parts = lax.all_to_all(
        out.reshape(groups * 2 * replicas, -1, width), ("hi", "lo", "rep"), 0, 0, tiled=True
    )
    parts = parts.reshape(groups, 2, replicas, -1, width).astype(F32)
    if halved(share):
        return jnp.sum(parts, axis=0).swapaxes(0, 1).reshape(rows, width).astype(BF16)
    return jnp.sum(parts, axis=(0, 1)).reshape(rows, width).astype(BF16)


def solution(mesh):
    replicas, tp = mesh.shape["rep"], mesh.shape["tp"]
    split = Mesh(mesh.devices.reshape(replicas, tp // 2, 2), ("rep", "hi", "lo"))
    cols = ("hi", "lo")
    in_specs = (
        P("rep", cols),
        P(),
        P(),
        P(None, cols),
        P(None, cols),
        P(None, cols),
        P(cols, None),
        P(None, cols),
        P(cols, None),
        P(None, cols),
        P("rep", None, cols),
        P("rep", None, cols),
        P(None, "rep"),
        P(None, "rep"),
        P("rep", None),
    )
    return jax.shard_map(
        functools.partial(on_device, replicas),
        mesh=split,
        in_specs=in_specs,
        out_specs=P("rep", cols),
        check_vma=False,
    )
```

```python
import functools

import jax
import jax.numpy as jnp
from jax import lax
from jax.experimental import pallas as pl
from jax.experimental.pallas import tpu as pltpu
from jax.sharding import Mesh, PartitionSpec as P

EPSILON = 1e-06
THRESHOLDS = (1, 2, 3, 4, 5, 6, 7, 8, 12, 16, 23, 32, 46, 64, 91)
BF16 = jnp.bfloat16
F32 = jnp.float32
VMEM = pl.BlockSpec(memory_space=pltpu.VMEM)
SMEM = pl.BlockSpec(memory_space=pltpu.SMEM)
PREPARE_FLOPS = 7 * 10**9
INNER_FLOPS = 40 * 10**9
LANES = 128
VMEM_LIMIT = 24 * 1024 * 1024


def dot(a, b):
    return jnp.dot(a, b, preferred_element_type=F32)


def place():
    upper, lower = lax.axis_index("hi"), lax.axis_index("lo")
    return upper * 2 + lower, lower


def halved(share):
    return share % 2 == 0


def columns_of(index, width):
    return pl.ds(pl.multiple_of(index * width, width), width)


def bias_of(table_ref, relative, head):
    distance = jnp.abs(relative)
    before = jnp.full(relative.shape, table_ref[head, 0], F32)
    after = jnp.full(relative.shape, table_ref[head, 17], F32)
    for step, threshold in enumerate(THRESHOLDS):
        far = distance >= threshold
        before = jnp.where(far, table_ref[head, step + 1], before)
        after = jnp.where(far, table_ref[head, step + 17], after)
    return jnp.where(relative > 0, after, before)


def prepare_kernel(
    replicas, cached, table_ref, counts_ref, lengths_ref, deal_ref, bias_ref, picked_ref
):
    _, side = place()
    rows = deal_ref.shape[1]
    new_slots = rows // 2
    half, share = rows // 2, rows // replicas
    deal = deal_ref[...]
    slot = lax.rem(deal, replicas) * share + lax.div(deal, replicas)
    lane = lax.broadcasted_iota(jnp.int32, (1, rows), 1)
    live = lane < jnp.where(
        lane < new_slots, counts_ref[0, 0], jnp.minimum(counts_ref[0, 1], new_slots) + new_slots
    )
    slot = jnp.where(live, slot, -1)
    row = lax.broadcasted_iota(jnp.int32, (rows, rows), 0)
    part = jnp.where(row < half, side, 1 - side)
    row = jnp.where(row < half, row, row - half)
    if halved(share):
        row = lax.div(row, share // 2) * share + part * (share // 2) + lax.rem(row, share // 2)
    else:
        row = part * half + row
    picked_ref[...] = jnp.where(row == slot, 1.0, 0.0).astype(BF16)

    requests, _, key_slots = bias_ref.shape
    key_index = lax.broadcasted_iota(jnp.int32, (new_slots, key_slots), 1)
    query_index = lax.broadcasted_iota(jnp.int32, (new_slots, key_slots), 0)
    is_cache = key_index < cached
    for j in range(requests):
        length, count = lengths_ref[0, j], counts_ref[0, j]
        position = jnp.where(is_cache, key_index, length + key_index - cached)
        relative = position - (length + query_index)
        live = jnp.where(is_cache, key_index - length, key_index - cached - count) < 0
        for h in range(table_ref.shape[0]):
            bias = jnp.where(live, bias_of(table_ref, relative, h), -1e30)
            bias_ref[j, h * new_slots : (h + 1) * new_slots] = bias


def attend(query, new_keys, new_values, old_keys, old_values, bias):
    new_slots, local_width = query.shape
    head_count = bias.shape[0] // new_slots
    lane = lax.broadcasted_iota(jnp.int32, (new_slots, local_width), 1)
    lane_head = lane // (local_width // head_count)
    stacked = jnp.concatenate(
        [jnp.where(lane_head == h, query, jnp.zeros_like(query)) for h in range(head_count)],
        axis=0,
    )
    keys = jnp.concatenate([old_keys, new_keys], axis=0)
    values = jnp.concatenate([old_values, new_values], axis=0)
    scores = lax.dot_general(stacked, keys, (((1,), (1,)), ((), ())), preferred_element_type=F32)
    scores = scores + bias
    weights = jnp.exp(scores - jnp.max(scores, axis=1, keepdims=True))
    probs = (weights / jnp.sum(weights, axis=1, keepdims=True)).astype(BF16)
    mixed = dot(probs, values)
    context = jnp.zeros((new_slots, local_width), F32)
    for h in range(head_count):
        context = jnp.where(lane_head == h, mixed[h * new_slots : (h + 1) * new_slots], context)
    return context.astype(BF16)


def products(ref, columns, gain_ref, weight_refs):
    block = ref[...].astype(F32)
    scaled = (block * gain_ref[:, columns]).astype(BF16)
    return jnp.sum(block * block, axis=1, keepdims=True), [
        dot(scaled, weight_ref[columns, :]) for weight_ref in weight_refs
    ]


def early_kernel(
    own_ref,
    near_ref,
    across_ref,
    gain_ref,
    w_query_ref,
    w_key_ref,
    w_value_ref,
    w_out_ref,
    cache_keys_ref,
    cache_values_ref,
    squares_ref,
    query_ref,
    key_ref,
    value_ref,
):
    del w_out_ref, cache_keys_ref, cache_values_ref
    index, _ = place()
    width = own_ref.shape[1]
    squares, sums = 0.0, (0.0, 0.0, 0.0)
    for ref, xor in ((own_ref, 0), (near_ref, 1), (across_ref, 2)):
        square, more = products(
            ref, columns_of(index ^ xor, width), gain_ref, (w_query_ref, w_key_ref, w_value_ref)
        )
        squares, sums = squares + square, [a + b for a, b in zip(sums, more)]
    squares_ref[...] = jnp.broadcast_to(squares, squares_ref.shape)
    query_ref[...], key_ref[...], value_ref[...] = sums


def attend_kernel(
    far_ref,
    squares_ref,
    query_ref,
    key_ref,
    value_ref,
    gain_ref,
    w_query_ref,
    w_key_ref,
    w_value_ref,
    w_out_ref,
    cache_keys_ref,
    cache_values_ref,
    bias_ref,
    picked_ref,
    send_ref,
    context_ref,
):
    index, _ = place()
    rows, width = far_ref.shape
    requests = bias_ref.shape[0]
    new_slots, half = rows // requests, rows // 2
    squares, sums = products(
        far_ref, columns_of(index ^ 3, width), gain_ref, (w_query_ref, w_key_ref, w_value_ref)
    )
    squares = squares_ref[:, :1] + squares
    inverse = lax.rsqrt(squares / gain_ref.shape[1] + EPSILON)
    queries, new_keys, new_values = (
        ((ref[...] + more) * inverse).astype(BF16)
        for ref, more in zip((query_ref, key_ref, value_ref), sums)
    )
    contexts = []
    for j in range(requests):
        own = slice(j * new_slots, (j + 1) * new_slots)
        contexts.append(
            attend(
                queries[own],
                new_keys[own],
                new_values[own],
                cache_keys_ref[j],
                cache_values_ref[j],
                bias_ref[j],
            )
        )
    context = dot(picked_ref[...], jnp.concatenate(contexts, axis=0)).astype(BF16)
    send_ref[...] = dot(context[half:], w_out_ref[...]).astype(BF16)
    context_ref[...] = context[:half]


def project_kernel(context_ref, w_out_ref, keep_ref):
    keep_ref[...] = dot(context_ref[...], w_out_ref[...])


def stream_kernel(own_ref, near_ref, far_ref, across_ref, picked_ref, stream_ref):
    index, _ = place()
    width = own_ref.shape[1]
    picked = picked_ref[: stream_ref.shape[0]]
    for ref, xor in ((own_ref, 0), (near_ref, 1), (far_ref, 3), (across_ref, 2)):
        stream_ref[:, columns_of(index ^ xor, width)] = dot(picked, ref[...]).astype(BF16)


def inner_kernel(
    pair_ref,
    other_ref,
    stream_ref,
    gain_ref,
    w_inner_ref,
    mixed_ref,
    input_ref,
    inverse_ref,
    hidden_ref,
):
    mixed = pair_ref[...].astype(F32) + other_ref[...].astype(F32) + stream_ref[...].astype(F32)
    mixed_ref[...] = mixed
    square = jnp.sum(mixed * mixed, axis=1, keepdims=True)
    inverse = lax.rsqrt(square / mixed.shape[1] + EPSILON)
    inverse_ref[...] = jnp.broadcast_to(inverse, inverse_ref.shape)
    scaled = (mixed * gain_ref[...]).astype(BF16)
    input_ref[...] = scaled
    hidden_ref[...] = jnp.maximum(dot(scaled, w_inner_ref[...]) * inverse, 0.0).astype(BF16)


def outer_kernel(
    mixed_ref,
    input_ref,
    inverse_ref,
    own_hidden_ref,
    near_inner_ref,
    own_outer_ref,
    near_outer_ref,
    out_ref,
):
    upper = lax.axis_index("hi")
    width = out_ref.shape[2]
    hidden = dot(input_ref[...], near_inner_ref[...]) * inverse_ref[:, :1]
    hidden = jnp.maximum(hidden, 0.0).astype(BF16)
    for t in range(out_ref.shape[0]):
        columns = slice(t * width, (t + 1) * width)
        value = dot(own_hidden_ref[...], own_outer_ref[:, columns])
        value = value + dot(hidden, near_outer_ref[:, columns])
        value = value + jnp.where(upper == t // 2, mixed_ref[:, columns], 0.0)
        out_ref[t] = value.astype(BF16)


def swap(value, xor):
    return lax.ppermute(value, ("hi", "lo"), [(i, i ^ xor) for i in range(4)])


def on_device(
    replicas,
    tokens,
    attn_gain,
    ffn_gain,
    w_query,
    w_key,
    w_value,
    w_out,
    w_inner,
    w_outer,
    bias_table,
    cache_keys,
    cache_values,
    new_counts,
    cached_lengths,
    deal,
):
    rows, width = tokens.shape
    requests, cached, local_width = cache_keys.shape
    new_slots = rows // requests
    model_width = attn_gain.shape[0]
    head_count = bias_table.shape[1]
    groups = lax.axis_size("hi")
    _, side = place()
    shape = jax.ShapeDtypeStruct
    local = functools.partial(
        pl.pallas_call, compiler_params=pltpu.CompilerParams(vmem_limit_bytes=VMEM_LIMIT)
    )
    across, far = swap(tokens, 2), swap(tokens, 3)
    bias, picked = local(
        functools.partial(prepare_kernel, replicas, cached),
        out_shape=(
            shape((requests, head_count * new_slots, cached + new_slots), F32),
            shape((rows, rows), BF16),
        ),
        in_specs=[SMEM] * 3 + [VMEM],
        out_specs=(VMEM,) * 2,
        cost_estimate=pl.CostEstimate(flops=PREPARE_FLOPS, bytes_accessed=0, transcendentals=0),
        name="prepare",
    )(bias_table.T, new_counts.T, cached_lengths.T, deal)
    near = swap(tokens, 1)
    half = rows // 2
    gain = attn_gain.reshape(1, model_width)
    projections = (w_query, w_key, w_value)
    sums = local(
        early_kernel,
        out_shape=(shape((rows, LANES), F32),) + (shape((rows, local_width), F32),) * 3,
        in_specs=[VMEM] * 10,
        out_specs=(VMEM,) * 4,
        name="early",
    )(tokens, near, across, gain, *projections, w_out, cache_keys, cache_values)
    send, context = local(
        attend_kernel,
        out_shape=(shape((half, model_width), BF16), shape((half, local_width), BF16)),
        in_specs=[VMEM] * 14,
        out_specs=(VMEM,) * 2,
        name="attend",
    )(
        far,
        *sums,
        gain,
        *projections,
        w_out,
        cache_keys,
        cache_values,
        bias,
        picked,
    )
    keep = local(
        project_kernel,
        out_shape=shape((half, model_width), F32),
        in_specs=[VMEM] * 2,
        out_specs=VMEM,
        name="project",
    )(context, w_out)
    stream = local(
        stream_kernel,
        out_shape=shape((half, model_width), BF16),
        in_specs=[VMEM] * 5,
        out_specs=VMEM,
        name="stream",
    )(tokens, near, far, across, picked)
    pair = (keep + swap(send, 1).astype(F32)).astype(BF16)
    late_inner, late_outer, pair = lax.optimization_barrier((w_inner, w_outer, pair))
    ff_width = w_inner.shape[1]
    mixed, ffn_input, inverse, hidden = local(
        inner_kernel,
        out_shape=(
            shape((half, model_width), F32),
            shape((half, model_width), BF16),
            shape((half, LANES), F32),
            shape((half, ff_width), BF16),
        ),
        in_specs=[VMEM] * 5,
        out_specs=(VMEM,) * 4,
        cost_estimate=pl.CostEstimate(flops=INNER_FLOPS, bytes_accessed=0, transcendentals=0),
        name="inner",
    )(pair, swap(pair, 2), stream, ffn_gain.reshape(1, model_width), w_inner)
    out = local(
        outer_kernel,
        out_shape=shape((groups * 2, half, width), BF16),
        in_specs=[VMEM] * 7,
        out_specs=VMEM,
        name="outer",
    )(mixed, ffn_input, inverse, hidden, swap(late_inner, 1), w_outer, swap(late_outer, 1))
    share = rows // replicas
    if not halved(share):
        padded = jnp.zeros((groups * 2, rows, width), BF16)
        out = lax.dynamic_update_slice_in_dim(padded, out, side * half, 1)
    parts = lax.all_to_all(
        out.reshape(groups * 2 * replicas, -1, width), ("hi", "lo", "rep"), 0, 0, tiled=True
    )
    parts = parts.reshape(groups, 2, replicas, -1, width).astype(F32)
    if halved(share):
        return jnp.sum(parts, axis=0).swapaxes(0, 1).reshape(rows, width).astype(BF16)
    return jnp.sum(parts, axis=(0, 1)).reshape(rows, width).astype(BF16)


def solution(mesh):
    replicas, tp = mesh.shape["rep"], mesh.shape["tp"]
    split = Mesh(mesh.devices.reshape(replicas, tp // 2, 2), ("rep", "hi", "lo"))
    cols = ("hi", "lo")
    in_specs = (
        P("rep", cols),
        P(),
        P(),
        P(None, cols),
        P(None, cols),
        P(None, cols),
        P(cols, None),
        P(None, cols),
        P(cols, None),
        P(None, cols),
        P("rep", None, cols),
        P("rep", None, cols),
        P(None, "rep"),
        P(None, "rep"),
        P("rep", None),
    )
    return jax.shard_map(
        functools.partial(on_device, replicas),
        mesh=split,
        in_specs=in_specs,
        out_specs=P("rep", cols),
        check_vma=False,
    )
```

```python
import functools

import jax
import jax.numpy as jnp
from jax import lax
from jax.experimental import pallas as pl
from jax.experimental.pallas import tpu as pltpu
from jax.sharding import Mesh, PartitionSpec as P

EPSILON = 1e-06
THRESHOLDS = (1, 2, 3, 4, 5, 6, 7, 8, 12, 16, 23, 32, 46, 64, 91)
BF16 = jnp.bfloat16
F32 = jnp.float32
VMEM = pl.BlockSpec(memory_space=pltpu.VMEM)
SMEM = pl.BlockSpec(memory_space=pltpu.SMEM)
PREPARE_FLOPS = 7 * 10**9
INNER_FLOPS = 40 * 10**9
LANES = 128
VMEM_LIMIT = 24 * 1024 * 1024


def dot(a, b):
    return jnp.dot(a, b, preferred_element_type=F32)


def place():
    upper, lower = lax.axis_index("hi"), lax.axis_index("lo")
    return upper * 2 + lower, lower


def halved(share):
    return share % 2 == 0


def columns_of(index, width):
    return pl.ds(pl.multiple_of(index * width, width), width)


def bias_of(table_ref, relative, head):
    distance = jnp.abs(relative)
    before = jnp.full(relative.shape, table_ref[head, 0], F32)
    after = jnp.full(relative.shape, table_ref[head, 17], F32)
    for step, threshold in enumerate(THRESHOLDS):
        far = distance >= threshold
        before = jnp.where(far, table_ref[head, step + 1], before)
        after = jnp.where(far, table_ref[head, step + 17], after)
    return jnp.where(relative > 0, after, before)


def prepare_kernel(
    replicas, cached, table_ref, counts_ref, lengths_ref, deal_ref, bias_ref, picked_ref
):
    _, side = place()
    rows = deal_ref.shape[1]
    new_slots = rows // 2
    half, share = rows // 2, rows // replicas
    deal = deal_ref[...]
    slot = lax.rem(deal, replicas) * share + lax.div(deal, replicas)
    lane = lax.broadcasted_iota(jnp.int32, (1, rows), 1)
    live = lane < jnp.where(
        lane < new_slots, counts_ref[0, 0], jnp.minimum(counts_ref[0, 1], new_slots) + new_slots
    )
    slot = jnp.where(live, slot, -1)
    row = lax.broadcasted_iota(jnp.int32, (rows, rows), 0)
    part = jnp.where(row < half, side, 1 - side)
    row = jnp.where(row < half, row, row - half)
    if halved(share):
        row = lax.div(row, share // 2) * share + part * (share // 2) + lax.rem(row, share // 2)
    else:
        row = part * half + row
    picked_ref[...] = jnp.where(row == slot, 1.0, 0.0).astype(BF16)

    requests, _, key_slots = bias_ref.shape
    key_index = lax.broadcasted_iota(jnp.int32, (new_slots, key_slots), 1)
    query_index = lax.broadcasted_iota(jnp.int32, (new_slots, key_slots), 0)
    is_cache = key_index < cached
    for j in range(requests):
        length, count = lengths_ref[0, j], counts_ref[0, j]
        position = jnp.where(is_cache, key_index, length + key_index - cached)
        relative = position - (length + query_index)
        live = jnp.where(is_cache, key_index - length, key_index - cached - count) < 0
        for h in range(table_ref.shape[0]):
            bias = jnp.where(live, bias_of(table_ref, relative, h), -1e30)
            bias_ref[j, h * new_slots : (h + 1) * new_slots] = bias


def heads_of(shape, heads):
    return lax.broadcasted_iota(jnp.int32, shape, 1) // (shape[1] // heads)


def scores_of(query, keys, bias):
    heads = bias.shape[0] // query.shape[0]
    lane_head = heads_of(query.shape, heads)
    stacked = jnp.concatenate(
        [jnp.where(lane_head == h, query, jnp.zeros_like(query)) for h in range(heads)], axis=0
    )
    scores = lax.dot_general(stacked, keys, (((1,), (1,)), ((), ())), preferred_element_type=F32)
    return scores + bias


def context_of(scores, values, new_slots):
    weights = jnp.exp(scores - jnp.max(scores, axis=1, keepdims=True))
    probs = (weights / jnp.sum(weights, axis=1, keepdims=True)).astype(BF16)
    mixed = dot(probs, values)
    heads = scores.shape[0] // new_slots
    context = mixed[:new_slots]
    lane_head = heads_of(context.shape, heads)
    for h in range(1, heads):
        context = jnp.where(lane_head == h, mixed[h * new_slots : (h + 1) * new_slots], context)
    return context.astype(BF16)


def attend_kernel(
    own_ref,
    near_ref,
    far_ref,
    across_ref,
    gain_ref,
    w_query_ref,
    w_key_ref,
    w_value_ref,
    w_out_ref,
    cache_keys_ref,
    cache_values_ref,
    bias_ref,
    picked_ref,
    send_ref,
    context_ref,
    normed_ref,
):
    index, _ = place()
    rows, width = own_ref.shape
    model_width = gain_ref.shape[1]
    requests = bias_ref.shape[0]
    new_slots, half = rows // requests, rows // 2
    blocks = [(own_ref, 0), (near_ref, 1), (far_ref, 3), (across_ref, 2)]
    squares = 0.0
    for ref, _ in blocks:
        block = ref[...].astype(F32)
        squares = squares + jnp.sum(block * block, axis=1, keepdims=True)
    inverse = lax.rsqrt(squares / model_width + EPSILON)
    for ref, xor in blocks:
        columns = columns_of(index ^ xor, width)
        normed = ref[...].astype(F32) * inverse * gain_ref[:, columns]
        normed_ref[:, columns] = normed.astype(BF16)
    queries = dot(normed_ref[...], w_query_ref[...]).astype(BF16)
    new_keys = dot(normed_ref[...], w_key_ref[...]).astype(BF16)
    scores = []
    for j in range(requests):
        own = slice(j * new_slots, (j + 1) * new_slots)
        keys = jnp.concatenate([cache_keys_ref[j], new_keys[own]], axis=0)
        scores.append(scores_of(queries[own], keys, bias_ref[j]))
    new_values = dot(normed_ref[...], w_value_ref[...]).astype(BF16)
    contexts = []
    for j in range(requests):
        own = slice(j * new_slots, (j + 1) * new_slots)
        values = jnp.concatenate([cache_values_ref[j], new_values[own]], axis=0)
        contexts.append(context_of(scores[j], values, new_slots))
    context = jnp.concatenate(contexts, axis=0)
    context_ref[...] = context
    dealt = dot(picked_ref[half:], context).astype(BF16)
    send_ref[...] = dot(dealt, w_out_ref[...]).astype(BF16)


def project_kernel(context_ref, picked_ref, w_out_ref, keep_ref):
    dealt = dot(picked_ref[: keep_ref.shape[0]], context_ref[...]).astype(BF16)
    keep_ref[...] = dot(dealt, w_out_ref[...])


def stream_kernel(own_ref, near_ref, far_ref, across_ref, picked_ref, stream_ref):
    index, _ = place()
    width = own_ref.shape[1]
    picked = picked_ref[: stream_ref.shape[0]]
    for ref, xor in ((own_ref, 0), (near_ref, 1), (far_ref, 3), (across_ref, 2)):
        stream_ref[:, columns_of(index ^ xor, width)] = dot(picked, ref[...]).astype(BF16)


def inner_kernel(
    pair_ref,
    other_ref,
    stream_ref,
    gain_ref,
    w_inner_ref,
    mixed_ref,
    input_ref,
    inverse_ref,
    hidden_ref,
):
    mixed = pair_ref[...].astype(F32) + other_ref[...].astype(F32) + stream_ref[...].astype(F32)
    mixed_ref[...] = mixed
    square = jnp.sum(mixed * mixed, axis=1, keepdims=True)
    inverse = lax.rsqrt(square / mixed.shape[1] + EPSILON)
    inverse_ref[...] = jnp.broadcast_to(inverse, inverse_ref.shape)
    scaled = (mixed * gain_ref[...]).astype(BF16)
    input_ref[...] = scaled
    hidden_ref[...] = jnp.maximum(dot(scaled, w_inner_ref[...]) * inverse, 0.0).astype(BF16)


def outer_kernel(
    mixed_ref,
    input_ref,
    inverse_ref,
    own_hidden_ref,
    near_inner_ref,
    own_outer_ref,
    near_outer_ref,
    out_ref,
):
    upper = lax.axis_index("hi")
    width = out_ref.shape[2]
    hidden = dot(input_ref[...], near_inner_ref[...]) * inverse_ref[:, :1]
    hidden = jnp.maximum(hidden, 0.0).astype(BF16)
    for t in range(out_ref.shape[0]):
        columns = slice(t * width, (t + 1) * width)
        value = dot(own_hidden_ref[...], own_outer_ref[:, columns])
        value = value + dot(hidden, near_outer_ref[:, columns])
        value = value + jnp.where(upper == t // 2, mixed_ref[:, columns], 0.0)
        out_ref[t] = value.astype(BF16)


def swap(value, xor):
    return lax.ppermute(value, ("hi", "lo"), [(i, i ^ xor) for i in range(4)])


def on_device(
    replicas,
    tokens,
    attn_gain,
    ffn_gain,
    w_query,
    w_key,
    w_value,
    w_out,
    w_inner,
    w_outer,
    bias_table,
    cache_keys,
    cache_values,
    new_counts,
    cached_lengths,
    deal,
):
    rows, width = tokens.shape
    requests, cached, local_width = cache_keys.shape
    new_slots = rows // requests
    model_width = attn_gain.shape[0]
    head_count = bias_table.shape[1]
    groups = lax.axis_size("hi")
    _, side = place()
    shape = jax.ShapeDtypeStruct
    local = functools.partial(
        pl.pallas_call, compiler_params=pltpu.CompilerParams(vmem_limit_bytes=VMEM_LIMIT)
    )
    across, far = swap(tokens, 2), swap(tokens, 3)
    bias, picked = local(
        functools.partial(prepare_kernel, replicas, cached),
        out_shape=(
            shape((requests, head_count * new_slots, cached + new_slots), F32),
            shape((rows, rows), BF16),
        ),
        in_specs=[SMEM] * 3 + [VMEM],
        out_specs=(VMEM,) * 2,
        cost_estimate=pl.CostEstimate(flops=PREPARE_FLOPS, bytes_accessed=0, transcendentals=0),
        name="prepare",
    )(bias_table.T, new_counts.T, cached_lengths.T, deal)
    late, bias, picked = lax.optimization_barrier((tokens, bias, picked))
    blocks = (tokens, swap(late, 1), far, across)
    half = rows // 2
    send, context = local(
        attend_kernel,
        out_shape=(shape((half, model_width), BF16), shape((rows, local_width), BF16)),
        in_specs=[VMEM] * 13,
        out_specs=(VMEM,) * 2,
        scratch_shapes=[pltpu.VMEM((rows, model_width), BF16)],
        name="attend",
    )(
        *blocks,
        attn_gain.reshape(1, model_width),
        w_query,
        w_key,
        w_value,
        w_out,
        cache_keys,
        cache_values,
        bias,
        picked,
    )
    keep = local(
        project_kernel,
        out_shape=shape((half, model_width), F32),
        in_specs=[VMEM] * 3,
        out_specs=VMEM,
        name="project",
    )(context, picked, w_out)
    stream = local(
        stream_kernel,
        out_shape=shape((half, model_width), BF16),
        in_specs=[VMEM] * 5,
        out_specs=VMEM,
        name="stream",
    )(*blocks, picked)
    pair = (keep + swap(send, 1).astype(F32)).astype(BF16)
    late_inner, late_outer, pair = lax.optimization_barrier((w_inner, w_outer, pair))
    ff_width = w_inner.shape[1]
    mixed, ffn_input, inverse, hidden = local(
        inner_kernel,
        out_shape=(
            shape((half, model_width), F32),
            shape((half, model_width), BF16),
            shape((half, LANES), F32),
            shape((half, ff_width), BF16),
        ),
        in_specs=[VMEM] * 5,
        out_specs=(VMEM,) * 4,
        cost_estimate=pl.CostEstimate(flops=INNER_FLOPS, bytes_accessed=0, transcendentals=0),
        name="inner",
    )(pair, swap(pair, 2), stream, ffn_gain.reshape(1, model_width), w_inner)
    out = local(
        outer_kernel,
        out_shape=shape((groups * 2, half, width), BF16),
        in_specs=[VMEM] * 7,
        out_specs=VMEM,
        name="outer",
    )(mixed, ffn_input, inverse, hidden, swap(late_inner, 1), w_outer, swap(late_outer, 1))
    share = rows // replicas
    if not halved(share):
        padded = jnp.zeros((groups * 2, rows, width), BF16)
        out = lax.dynamic_update_slice_in_dim(padded, out, side * half, 1)
    parts = lax.all_to_all(
        out.reshape(groups * 2 * replicas, -1, width), ("hi", "lo", "rep"), 0, 0, tiled=True
    )
    parts = parts.reshape(groups, 2, replicas, -1, width).astype(F32)
    if halved(share):
        return jnp.sum(parts, axis=0).swapaxes(0, 1).reshape(rows, width).astype(BF16)
    return jnp.sum(parts, axis=(0, 1)).reshape(rows, width).astype(BF16)


def solution(mesh):
    replicas, tp = mesh.shape["rep"], mesh.shape["tp"]
    split = Mesh(mesh.devices.reshape(replicas, tp // 2, 2), ("rep", "hi", "lo"))
    cols = ("hi", "lo")
    in_specs = (
        P("rep", cols),
        P(),
        P(),
        P(None, cols),
        P(None, cols),
        P(None, cols),
        P(cols, None),
        P(None, cols),
        P(cols, None),
        P(None, cols),
        P("rep", None, cols),
        P("rep", None, cols),
        P(None, "rep"),
        P(None, "rep"),
        P("rep", None),
    )
    return jax.shard_map(
        functools.partial(on_device, replicas),
        mesh=split,
        in_specs=in_specs,
        out_specs=P("rep", cols),
        check_vma=False,
    )
```

```python
import functools

import jax
import jax.numpy as jnp
from jax import lax
from jax.experimental import pallas as pl
from jax.experimental.pallas import tpu as pltpu
from jax.sharding import Mesh, PartitionSpec as P

EPSILON = 1e-06
THRESHOLDS = (1, 2, 3, 4, 5, 6, 7, 8, 12, 16, 23, 32, 46, 64, 91)
BF16 = jnp.bfloat16
F32 = jnp.float32
VMEM = pl.BlockSpec(memory_space=pltpu.VMEM)
SMEM = pl.BlockSpec(memory_space=pltpu.SMEM)
PREPARE_FLOPS = 7 * 10**9
INNER_FLOPS = 40 * 10**9
LANES = 128
VMEM_LIMIT = 24 * 1024 * 1024


def dot(a, b):
    return jnp.dot(a, b, preferred_element_type=F32)


def place():
    upper, lower = lax.axis_index("hi"), lax.axis_index("lo")
    return upper * 2 + lower, lower


def halved(share):
    return share % 2 == 0


def columns_of(index, width):
    return pl.ds(pl.multiple_of(index * width, width), width)


def bias_of(table_ref, relative, head):
    distance = jnp.abs(relative)
    before = jnp.full(relative.shape, table_ref[head, 0], F32)
    after = jnp.full(relative.shape, table_ref[head, 17], F32)
    for step, threshold in enumerate(THRESHOLDS):
        far = distance >= threshold
        before = jnp.where(far, table_ref[head, step + 1], before)
        after = jnp.where(far, table_ref[head, step + 17], after)
    return jnp.where(relative > 0, after, before)


def prepare_kernel(
    replicas, cached, table_ref, counts_ref, lengths_ref, deal_ref, bias_ref, picked_ref
):
    _, side = place()
    rows = deal_ref.shape[1]
    new_slots = rows // 2
    half, share = rows // 2, rows // replicas
    deal = deal_ref[...]
    slot = lax.rem(deal, replicas) * share + lax.div(deal, replicas)
    lane = lax.broadcasted_iota(jnp.int32, (1, rows), 1)
    live = lane < jnp.where(
        lane < new_slots, counts_ref[0, 0], jnp.minimum(counts_ref[0, 1], new_slots) + new_slots
    )
    slot = jnp.where(live, slot, -1)
    row = lax.broadcasted_iota(jnp.int32, (rows, rows), 0)
    part = jnp.where(row < half, side, 1 - side)
    row = jnp.where(row < half, row, row - half)
    if halved(share):
        row = lax.div(row, share // 2) * share + part * (share // 2) + lax.rem(row, share // 2)
    else:
        row = part * half + row
    picked_ref[...] = jnp.where(row == slot, 1.0, 0.0).astype(BF16)

    requests, _, key_slots = bias_ref.shape
    key_index = lax.broadcasted_iota(jnp.int32, (new_slots, key_slots), 1)
    query_index = lax.broadcasted_iota(jnp.int32, (new_slots, key_slots), 0)
    is_cache = key_index < cached
    for j in range(requests):
        length, count = lengths_ref[0, j], counts_ref[0, j]
        position = jnp.where(is_cache, key_index, length + key_index - cached)
        relative = position - (length + query_index)
        live = jnp.where(is_cache, key_index - length, key_index - cached - count) < 0
        for h in range(table_ref.shape[0]):
            bias = jnp.where(live, bias_of(table_ref, relative, h), -1e30)
            bias_ref[j, h * new_slots : (h + 1) * new_slots] = bias


def heads_of(shape, heads):
    return lax.broadcasted_iota(jnp.int32, shape, 1) // (shape[1] // heads)


def scores_of(query, keys, bias):
    heads = bias.shape[0] // query.shape[0]
    lane_head = heads_of(query.shape, heads)
    stacked = jnp.concatenate(
        [jnp.where(lane_head == h, query, jnp.zeros_like(query)) for h in range(heads)], axis=0
    )
    scores = lax.dot_general(stacked, keys, (((1,), (1,)), ((), ())), preferred_element_type=F32)
    return scores + bias


def context_of(scores, values, new_slots):
    weights = jnp.exp(scores - jnp.max(scores, axis=1, keepdims=True))
    mixed = dot(weights.astype(BF16), values) / jnp.sum(weights, axis=1, keepdims=True)
    heads = scores.shape[0] // new_slots
    context = mixed[:new_slots]
    lane_head = heads_of(context.shape, heads)
    for h in range(1, heads):
        context = jnp.where(lane_head == h, mixed[h * new_slots : (h + 1) * new_slots], context)
    return context.astype(BF16)


def attend_kernel(
    own_ref,
    near_ref,
    far_ref,
    across_ref,
    gain_ref,
    w_query_ref,
    w_key_ref,
    w_value_ref,
    cache_keys_ref,
    cache_values_ref,
    bias_ref,
    picked_ref,
    send_ref,
    context_ref,
    normed_ref,
):
    index, _ = place()
    rows, width = own_ref.shape
    model_width = gain_ref.shape[1]
    requests = bias_ref.shape[0]
    new_slots, half = rows // requests, rows // 2
    blocks = [(own_ref, 0), (near_ref, 1), (far_ref, 3), (across_ref, 2)]
    squares = 0.0
    for ref, _ in blocks:
        block = ref[...].astype(F32)
        squares = squares + jnp.sum(block * block, axis=1, keepdims=True)
    inverse = lax.rsqrt(squares / model_width + EPSILON)
    for ref, xor in blocks:
        columns = columns_of(index ^ xor, width)
        normed = ref[...].astype(F32) * inverse * gain_ref[:, columns]
        normed_ref[:, columns] = normed.astype(BF16)
    queries = dot(normed_ref[...], w_query_ref[...]).astype(BF16)
    new_keys = dot(normed_ref[...], w_key_ref[...]).astype(BF16)
    scores = []
    for j in range(requests):
        own = slice(j * new_slots, (j + 1) * new_slots)
        keys = jnp.concatenate([cache_keys_ref[j], new_keys[own]], axis=0)
        scores.append(scores_of(queries[own], keys, bias_ref[j]))
    new_values = dot(normed_ref[...], w_value_ref[...]).astype(BF16)
    contexts = []
    for j in range(requests):
        own = slice(j * new_slots, (j + 1) * new_slots)
        values = jnp.concatenate([cache_values_ref[j], new_values[own]], axis=0)
        contexts.append(context_of(scores[j], values, new_slots))
    context = jnp.concatenate(contexts, axis=0)
    context_ref[...] = context
    send_ref[...] = dot(picked_ref[half:], context).astype(BF16)


def project_kernel(context_ref, picked_ref, w_out_ref, keep_ref):
    dealt = dot(picked_ref[: keep_ref.shape[0]], context_ref[...]).astype(BF16)
    keep_ref[...] = dot(dealt, w_out_ref[...])


def pair_kernel(keep_ref, near_ref, near_out_ref, pair_ref):
    pair_ref[...] = (keep_ref[...] + dot(near_ref[...], near_out_ref[...])).astype(BF16)


def stream_kernel(own_ref, near_ref, far_ref, across_ref, picked_ref, stream_ref):
    index, _ = place()
    width = own_ref.shape[1]
    picked = picked_ref[: stream_ref.shape[0]]
    for ref, xor in ((own_ref, 0), (near_ref, 1), (far_ref, 3), (across_ref, 2)):
        stream_ref[:, columns_of(index ^ xor, width)] = dot(picked, ref[...]).astype(BF16)


def inner_kernel(
    pair_ref,
    other_ref,
    stream_ref,
    gain_ref,
    w_inner_ref,
    mixed_ref,
    input_ref,
    inverse_ref,
    hidden_ref,
):
    mixed = pair_ref[...].astype(F32) + other_ref[...].astype(F32) + stream_ref[...].astype(F32)
    mixed_ref[...] = mixed
    square = jnp.sum(mixed * mixed, axis=1, keepdims=True)
    inverse = lax.rsqrt(square / mixed.shape[1] + EPSILON)
    inverse_ref[...] = jnp.broadcast_to(inverse, inverse_ref.shape)
    scaled = (mixed * gain_ref[...]).astype(BF16)
    input_ref[...] = scaled
    hidden_ref[...] = jnp.maximum(dot(scaled, w_inner_ref[...]) * inverse, 0.0).astype(BF16)


def outer_kernel(
    mixed_ref,
    input_ref,
    inverse_ref,
    own_hidden_ref,
    near_inner_ref,
    own_outer_ref,
    near_outer_ref,
    out_ref,
):
    upper = lax.axis_index("hi")
    width = out_ref.shape[2]
    hidden = dot(input_ref[...], near_inner_ref[...]) * inverse_ref[:, :1]
    hidden = jnp.maximum(hidden, 0.0).astype(BF16)
    for t in range(out_ref.shape[0]):
        columns = slice(t * width, (t + 1) * width)
        value = dot(own_hidden_ref[...], own_outer_ref[:, columns])
        value = value + dot(hidden, near_outer_ref[:, columns])
        value = value + jnp.where(upper == t // 2, mixed_ref[:, columns], 0.0)
        out_ref[t] = value.astype(BF16)


def swap(value, xor):
    return lax.ppermute(value, ("hi", "lo"), [(i, i ^ xor) for i in range(4)])


def on_device(
    replicas,
    tokens,
    attn_gain,
    ffn_gain,
    w_query,
    w_key,
    w_value,
    w_out,
    w_inner,
    w_outer,
    bias_table,
    cache_keys,
    cache_values,
    new_counts,
    cached_lengths,
    deal,
):
    rows, width = tokens.shape
    requests, cached, local_width = cache_keys.shape
    new_slots = rows // requests
    model_width = attn_gain.shape[0]
    head_count = bias_table.shape[1]
    groups = lax.axis_size("hi")
    _, side = place()
    shape = jax.ShapeDtypeStruct
    local = functools.partial(
        pl.pallas_call, compiler_params=pltpu.CompilerParams(vmem_limit_bytes=VMEM_LIMIT)
    )
    across, far = swap(tokens, 2), swap(tokens, 3)
    bias, picked = local(
        functools.partial(prepare_kernel, replicas, cached),
        out_shape=(
            shape((requests, head_count * new_slots, cached + new_slots), F32),
            shape((rows, rows), BF16),
        ),
        in_specs=[SMEM] * 3 + [VMEM],
        out_specs=(VMEM,) * 2,
        cost_estimate=pl.CostEstimate(flops=PREPARE_FLOPS, bytes_accessed=0, transcendentals=0),
        name="prepare",
    )(bias_table.T, new_counts.T, cached_lengths.T, deal)
    late, bias, picked = lax.optimization_barrier((tokens, bias, picked))
    blocks = (tokens, swap(late, 1), far, across)
    half = rows // 2
    send, context = local(
        attend_kernel,
        out_shape=(shape((half, local_width), BF16), shape((rows, local_width), BF16)),
        in_specs=[VMEM] * 12,
        out_specs=(VMEM,) * 2,
        scratch_shapes=[pltpu.VMEM((rows, model_width), BF16)],
        cost_estimate=pl.CostEstimate(flops=INNER_FLOPS, bytes_accessed=0, transcendentals=0),
        name="attend",
    )(
        *blocks,
        attn_gain.reshape(1, model_width),
        w_query,
        w_key,
        w_value,
        cache_keys,
        cache_values,
        bias,
        picked,
    )
    keep = local(
        project_kernel,
        out_shape=shape((half, model_width), F32),
        in_specs=[VMEM] * 3,
        out_specs=VMEM,
        name="project",
    )(context, picked, w_out)
    stream = local(
        stream_kernel,
        out_shape=shape((half, model_width), BF16),
        in_specs=[VMEM] * 5,
        out_specs=VMEM,
        name="stream",
    )(*blocks, picked)
    pair = local(
        pair_kernel,
        out_shape=shape((half, model_width), BF16),
        in_specs=[VMEM] * 3,
        out_specs=VMEM,
        name="pair",
    )(keep, swap(send, 1), swap(w_out, 1))
    late_inner, late_outer, pair = lax.optimization_barrier((w_inner, w_outer, pair))
    ff_width = w_inner.shape[1]
    mixed, ffn_input, inverse, hidden = local(
        inner_kernel,
        out_shape=(
            shape((half, model_width), F32),
            shape((half, model_width), BF16),
            shape((half, LANES), F32),
            shape((half, ff_width), BF16),
        ),
        in_specs=[VMEM] * 5,
        out_specs=(VMEM,) * 4,
        cost_estimate=pl.CostEstimate(flops=INNER_FLOPS, bytes_accessed=0, transcendentals=0),
        name="inner",
    )(pair, swap(pair, 2), stream, ffn_gain.reshape(1, model_width), w_inner)
    out = local(
        outer_kernel,
        out_shape=shape((groups * 2, half, width), BF16),
        in_specs=[VMEM] * 7,
        out_specs=VMEM,
        name="outer",
    )(mixed, ffn_input, inverse, hidden, swap(late_inner, 1), w_outer, swap(late_outer, 1))
    share = rows // replicas
    if not halved(share):
        padded = jnp.zeros((groups * 2, rows, width), BF16)
        out = lax.dynamic_update_slice_in_dim(padded, out, side * half, 1)
    parts = lax.all_to_all(
        out.reshape(groups * 2 * replicas, -1, width), ("hi", "lo", "rep"), 0, 0, tiled=True
    )
    parts = parts.reshape(groups, 2, replicas, -1, width).astype(F32)
    if halved(share):
        return jnp.sum(parts, axis=0).swapaxes(0, 1).reshape(rows, width).astype(BF16)
    return jnp.sum(parts, axis=(0, 1)).reshape(rows, width).astype(BF16)


def solution(mesh):
    replicas, tp = mesh.shape["rep"], mesh.shape["tp"]
    split = Mesh(mesh.devices.reshape(replicas, tp // 2, 2), ("rep", "hi", "lo"))
    cols = ("hi", "lo")
    in_specs = (
        P("rep", cols),
        P(),
        P(),
        P(None, cols),
        P(None, cols),
        P(None, cols),
        P(cols, None),
        P(None, cols),
        P(cols, None),
        P(None, cols),
        P("rep", None, cols),
        P("rep", None, cols),
        P(None, "rep"),
        P(None, "rep"),
        P("rep", None),
    )
    return jax.shard_map(
        functools.partial(on_device, replicas),
        mesh=split,
        in_specs=in_specs,
        out_specs=P("rep", cols),
        check_vma=False,
    )
```

```python
import functools

import jax
import jax.numpy as jnp
from jax import lax
from jax.experimental import pallas as pl
from jax.experimental.pallas import tpu as pltpu
from jax.sharding import Mesh, PartitionSpec as P

EPSILON = 1e-06
THRESHOLDS = (1, 2, 3, 4, 5, 6, 7, 8, 12, 16, 23, 32, 46, 64, 91)
BF16 = jnp.bfloat16
F32 = jnp.float32
VMEM = pl.BlockSpec(memory_space=pltpu.VMEM)
SMEM = pl.BlockSpec(memory_space=pltpu.SMEM)
PREPARE_FLOPS = 7 * 10**9
INNER_FLOPS = 40 * 10**9
LANES = 128
VMEM_LIMIT = 24 * 1024 * 1024


def dot(a, b):
    return jnp.dot(a, b, preferred_element_type=F32)


def place():
    upper, lower = lax.axis_index("hi"), lax.axis_index("lo")
    return upper * 2 + lower, lower


def halved(share):
    return share % 2 == 0


def columns_of(index, width):
    return pl.ds(pl.multiple_of(index * width, width), width)


def bias_of(table_ref, relative, head):
    distance = jnp.abs(relative)
    before = jnp.full(relative.shape, table_ref[head, 0], F32)
    after = jnp.full(relative.shape, table_ref[head, 17], F32)
    for step, threshold in enumerate(THRESHOLDS):
        far = distance >= threshold
        before = jnp.where(far, table_ref[head, step + 1], before)
        after = jnp.where(far, table_ref[head, step + 17], after)
    return jnp.where(relative > 0, after, before)


def prepare_kernel(
    replicas, cached, table_ref, counts_ref, lengths_ref, deal_ref, bias_ref, picked_ref
):
    _, side = place()
    rows = deal_ref.shape[1]
    new_slots = rows // 2
    half, share = rows // 2, rows // replicas
    deal = deal_ref[...]
    slot = lax.rem(deal, replicas) * share + lax.div(deal, replicas)
    lane = lax.broadcasted_iota(jnp.int32, (1, rows), 1)
    live = lane < jnp.where(
        lane < new_slots, counts_ref[0, 0], jnp.minimum(counts_ref[0, 1], new_slots) + new_slots
    )
    slot = jnp.where(live, slot, -1)
    row = lax.broadcasted_iota(jnp.int32, (rows, rows), 0)
    part = jnp.where(row < half, side, 1 - side)
    row = jnp.where(row < half, row, row - half)
    if halved(share):
        row = lax.div(row, share // 2) * share + part * (share // 2) + lax.rem(row, share // 2)
    else:
        row = part * half + row
    picked_ref[...] = jnp.where(row == slot, 1.0, 0.0).astype(BF16)

    requests, _, key_slots = bias_ref.shape
    key_index = lax.broadcasted_iota(jnp.int32, (new_slots, key_slots), 1)
    query_index = lax.broadcasted_iota(jnp.int32, (new_slots, key_slots), 0)
    is_cache = key_index < cached
    for j in range(requests):
        length, count = lengths_ref[0, j], counts_ref[0, j]
        position = jnp.where(is_cache, key_index, length + key_index - cached)
        relative = position - (length + query_index)
        live = jnp.where(is_cache, key_index - length, key_index - cached - count) < 0
        for h in range(table_ref.shape[0]):
            bias = jnp.where(live, bias_of(table_ref, relative, h), -1e30)
            bias_ref[j, h * new_slots : (h + 1) * new_slots] = bias


def heads_of(shape, heads):
    return lax.broadcasted_iota(jnp.int32, shape, 1) // (shape[1] // heads)


def scores_of(query, keys, bias):
    heads = bias.shape[0] // query.shape[0]
    lane_head = heads_of(query.shape, heads)
    stacked = jnp.concatenate(
        [jnp.where(lane_head == h, query, jnp.zeros_like(query)) for h in range(heads)], axis=0
    )
    scores = lax.dot_general(stacked, keys, (((1,), (1,)), ((), ())), preferred_element_type=F32)
    return scores + bias


def context_of(scores, values, new_slots):
    weights = jnp.exp(scores - jnp.max(scores, axis=1, keepdims=True))
    mixed = dot(weights.astype(BF16), values) / jnp.sum(weights, axis=1, keepdims=True)
    heads = scores.shape[0] // new_slots
    context = mixed[:new_slots]
    lane_head = heads_of(context.shape, heads)
    for h in range(1, heads):
        context = jnp.where(lane_head == h, mixed[h * new_slots : (h + 1) * new_slots], context)
    return context.astype(BF16)


def attend_kernel(
    own_ref,
    far_ref,
    near_ref,
    across_ref,
    gain_ref,
    w_query_ref,
    w_key_ref,
    w_value_ref,
    cache_keys_ref,
    cache_values_ref,
    bias_ref,
    picked_ref,
    send_ref,
    context_ref,
    normed_ref,
):
    index, _ = place()
    rows, width = own_ref.shape
    model_width = gain_ref.shape[1]
    requests = bias_ref.shape[0]
    new_slots, half = rows // requests, rows // 2
    blocks = [(own_ref, 0), (near_ref, 1), (far_ref, 3), (across_ref, 2)]
    squares = 0.0
    for ref, _ in blocks:
        block = ref[...].astype(F32)
        squares = squares + jnp.sum(block * block, axis=1, keepdims=True)
    inverse = lax.rsqrt(squares / model_width + EPSILON)
    for ref, xor in blocks:
        columns = columns_of(index ^ xor, width)
        normed = ref[...].astype(F32) * inverse * gain_ref[:, columns]
        normed_ref[:, columns] = normed.astype(BF16)
    queries = dot(normed_ref[...], w_query_ref[...]).astype(BF16)
    new_keys = dot(normed_ref[...], w_key_ref[...]).astype(BF16)
    scores = []
    for j in range(requests):
        own = slice(j * new_slots, (j + 1) * new_slots)
        keys = jnp.concatenate([cache_keys_ref[j], new_keys[own]], axis=0)
        scores.append(scores_of(queries[own], keys, bias_ref[j]))
    new_values = dot(normed_ref[...], w_value_ref[...]).astype(BF16)
    contexts = []
    for j in range(requests):
        own = slice(j * new_slots, (j + 1) * new_slots)
        values = jnp.concatenate([cache_values_ref[j], new_values[own]], axis=0)
        contexts.append(context_of(scores[j], values, new_slots))
    context = jnp.concatenate(contexts, axis=0)
    context_ref[...] = context
    send_ref[...] = dot(picked_ref[half:], context).astype(BF16)


def project_kernel(context_ref, picked_ref, w_out_ref, keep_ref):
    dealt = dot(picked_ref[: keep_ref.shape[0]], context_ref[...]).astype(BF16)
    keep_ref[...] = dot(dealt, w_out_ref[...])


def pair_kernel(keep_ref, near_ref, near_out_ref, near_inner_ref, pair_ref):
    del near_inner_ref
    pair_ref[...] = (keep_ref[...] + dot(near_ref[...], near_out_ref[...])).astype(BF16)


def stream_kernel(own_ref, far_ref, near_ref, across_ref, picked_ref, stream_ref):
    index, _ = place()
    width = own_ref.shape[1]
    picked = picked_ref[: stream_ref.shape[0]]
    for ref, xor in ((own_ref, 0), (near_ref, 1), (far_ref, 3), (across_ref, 2)):
        stream_ref[:, columns_of(index ^ xor, width)] = dot(picked, ref[...]).astype(BF16)


def inner_kernel(
    pair_ref,
    other_ref,
    stream_ref,
    gain_ref,
    w_inner_ref,
    mixed_ref,
    input_ref,
    inverse_ref,
    hidden_ref,
):
    mixed = pair_ref[...].astype(F32) + other_ref[...].astype(F32) + stream_ref[...].astype(F32)
    mixed_ref[...] = mixed
    square = jnp.sum(mixed * mixed, axis=1, keepdims=True)
    inverse = lax.rsqrt(square / mixed.shape[1] + EPSILON)
    inverse_ref[...] = jnp.broadcast_to(inverse, inverse_ref.shape)
    scaled = (mixed * gain_ref[...]).astype(BF16)
    input_ref[...] = scaled
    hidden_ref[...] = jnp.maximum(dot(scaled, w_inner_ref[...]) * inverse, 0.0).astype(BF16)


def outer_kernel(
    mixed_ref,
    input_ref,
    inverse_ref,
    own_hidden_ref,
    near_inner_ref,
    own_outer_ref,
    near_outer_ref,
    out_ref,
):
    upper = lax.axis_index("hi")
    width = out_ref.shape[2]
    hidden = dot(input_ref[...], near_inner_ref[...]) * inverse_ref[:, :1]
    hidden = jnp.maximum(hidden, 0.0).astype(BF16)
    for t in range(out_ref.shape[0]):
        columns = slice(t * width, (t + 1) * width)
        value = dot(own_hidden_ref[...], own_outer_ref[:, columns])
        value = value + dot(hidden, near_outer_ref[:, columns])
        value = value + jnp.where(upper == t // 2, mixed_ref[:, columns], 0.0)
        out_ref[t] = value.astype(BF16)


def swap(value, xor):
    return lax.ppermute(value, ("hi", "lo"), [(i, i ^ xor) for i in range(4)])


def on_device(
    replicas,
    tokens,
    attn_gain,
    ffn_gain,
    w_query,
    w_key,
    w_value,
    w_out,
    w_inner,
    w_outer,
    bias_table,
    cache_keys,
    cache_values,
    new_counts,
    cached_lengths,
    deal,
):
    rows, width = tokens.shape
    requests, cached, local_width = cache_keys.shape
    new_slots = rows // requests
    model_width = attn_gain.shape[0]
    head_count = bias_table.shape[1]
    groups = lax.axis_size("hi")
    _, side = place()
    shape = jax.ShapeDtypeStruct
    local = functools.partial(
        pl.pallas_call, compiler_params=pltpu.CompilerParams(vmem_limit_bytes=VMEM_LIMIT)
    )
    across, far = swap(tokens, 2), swap(tokens, 3)
    bias, picked = local(
        functools.partial(prepare_kernel, replicas, cached),
        out_shape=(
            shape((requests, head_count * new_slots, cached + new_slots), F32),
            shape((rows, rows), BF16),
        ),
        in_specs=[SMEM] * 3 + [VMEM],
        out_specs=(VMEM,) * 2,
        cost_estimate=pl.CostEstimate(flops=PREPARE_FLOPS, bytes_accessed=0, transcendentals=0),
        name="prepare",
    )(bias_table.T, new_counts.T, cached_lengths.T, deal)
    blocks = (tokens, far, swap(tokens, 1), across)
    half = rows // 2
    send, context = local(
        attend_kernel,
        out_shape=(shape((half, local_width), BF16), shape((rows, local_width), BF16)),
        in_specs=[VMEM] * 12,
        out_specs=(VMEM,) * 2,
        scratch_shapes=[pltpu.VMEM((rows, model_width), BF16)],
        cost_estimate=pl.CostEstimate(flops=INNER_FLOPS, bytes_accessed=0, transcendentals=0),
        name="attend",
    )(
        *blocks,
        attn_gain.reshape(1, model_width),
        w_query,
        w_key,
        w_value,
        cache_keys,
        cache_values,
        bias,
        picked,
    )
    keep = local(
        project_kernel,
        out_shape=shape((half, model_width), F32),
        in_specs=[VMEM] * 3,
        out_specs=VMEM,
        name="project",
    )(context, picked, w_out)
    stream = local(
        stream_kernel,
        out_shape=shape((half, model_width), BF16),
        in_specs=[VMEM] * 5,
        out_specs=VMEM,
        name="stream",
    )(*blocks, picked)
    near_inner = swap(w_inner, 1)
    pair = local(
        pair_kernel,
        out_shape=shape((half, model_width), BF16),
        in_specs=[VMEM] * 4,
        out_specs=VMEM,
        name="pair",
    )(keep, swap(send, 1), swap(w_out, 1), near_inner)
    late_outer, pair = lax.optimization_barrier((w_outer, pair))
    ff_width = w_inner.shape[1]
    mixed, ffn_input, inverse, hidden = local(
        inner_kernel,
        out_shape=(
            shape((half, model_width), F32),
            shape((half, model_width), BF16),
            shape((half, LANES), F32),
            shape((half, ff_width), BF16),
        ),
        in_specs=[VMEM] * 5,
        out_specs=(VMEM,) * 4,
        cost_estimate=pl.CostEstimate(flops=INNER_FLOPS, bytes_accessed=0, transcendentals=0),
        name="inner",
    )(pair, swap(pair, 2), stream, ffn_gain.reshape(1, model_width), w_inner)
    out = local(
        outer_kernel,
        out_shape=shape((groups * 2, half, width), BF16),
        in_specs=[VMEM] * 7,
        out_specs=VMEM,
        name="outer",
    )(mixed, ffn_input, inverse, hidden, near_inner, w_outer, swap(late_outer, 1))
    share = rows // replicas
    if not halved(share):
        padded = jnp.zeros((groups * 2, rows, width), BF16)
        out = lax.dynamic_update_slice_in_dim(padded, out, side * half, 1)
    parts = lax.all_to_all(
        out.reshape(groups * 2 * replicas, -1, width), ("hi", "lo", "rep"), 0, 0, tiled=True
    )
    parts = parts.reshape(groups, 2, replicas, -1, width).astype(F32)
    if halved(share):
        return jnp.sum(parts, axis=0).swapaxes(0, 1).reshape(rows, width).astype(BF16)
    return jnp.sum(parts, axis=(0, 1)).reshape(rows, width).astype(BF16)


def solution(mesh):
    replicas, tp = mesh.shape["rep"], mesh.shape["tp"]
    split = Mesh(mesh.devices.reshape(replicas, tp // 2, 2), ("rep", "hi", "lo"))
    cols = ("hi", "lo")
    in_specs = (
        P("rep", cols),
        P(),
        P(),
        P(None, cols),
        P(None, cols),
        P(None, cols),
        P(cols, None),
        P(None, cols),
        P(cols, None),
        P(None, cols),
        P("rep", None, cols),
        P("rep", None, cols),
        P(None, "rep"),
        P(None, "rep"),
        P("rep", None),
    )
    return jax.shard_map(
        functools.partial(on_device, replicas),
        mesh=split,
        in_specs=in_specs,
        out_specs=P("rep", cols),
        check_vma=False,
    )
```

```python
import functools

import jax
import jax.numpy as jnp
from jax import lax
from jax.experimental import pallas as pl
from jax.experimental.pallas import tpu as pltpu
from jax.sharding import Mesh, PartitionSpec as P

EPSILON = 1e-06
THRESHOLDS = (1, 2, 3, 4, 5, 6, 7, 8, 12, 16, 23, 32, 46, 64, 91)
BF16 = jnp.bfloat16
F32 = jnp.float32
VMEM = pl.BlockSpec(memory_space=pltpu.VMEM)
SMEM = pl.BlockSpec(memory_space=pltpu.SMEM)
PREPARE_FLOPS = 7 * 10**9
INNER_FLOPS = 40 * 10**9
LANES = 128
VMEM_LIMIT = 24 * 1024 * 1024


def dot(a, b):
    return jnp.dot(a, b, preferred_element_type=F32)


def place():
    upper, lower = lax.axis_index("hi"), lax.axis_index("lo")
    return upper * 2 + lower, lower


def straight(replicas, share):
    return replicas * 3 // 4 if halved(share) and replicas % 4 == 0 else replicas


def halved(share):
    return share % 2 == 0


def columns_of(index, width):
    return pl.ds(pl.multiple_of(index * width, width), width)


def bias_of(table_ref, relative, head):
    distance = jnp.abs(relative)
    before = jnp.full(relative.shape, table_ref[head, 0], F32)
    after = jnp.full(relative.shape, table_ref[head, 17], F32)
    for step, threshold in enumerate(THRESHOLDS):
        far = distance >= threshold
        before = jnp.where(far, table_ref[head, step + 1], before)
        after = jnp.where(far, table_ref[head, step + 17], after)
    return jnp.where(relative > 0, after, before)


def prepare_kernel(
    replicas, cached, table_ref, counts_ref, lengths_ref, deal_ref, bias_ref, picked_ref
):
    _, side = place()
    rows = deal_ref.shape[1]
    new_slots = rows // 2
    half, share = rows // 2, rows // replicas
    deal = deal_ref[...]
    slot = lax.rem(deal, replicas) * share + lax.div(deal, replicas)
    lane = lax.broadcasted_iota(jnp.int32, (1, rows), 1)
    live = lane < jnp.where(
        lane < new_slots, counts_ref[0, 0], jnp.minimum(counts_ref[0, 1], new_slots) + new_slots
    )
    slot = jnp.where(live, slot, -1)
    row = lax.broadcasted_iota(jnp.int32, (rows, rows), 0)
    part = jnp.where(row < half, side, 1 - side)
    row = jnp.where(row < half, row, row - half)
    crossed = row >= jnp.where(lax.axis_index("hi") == 0, half, straight(replicas, share) * half // replicas)
    part = jnp.where(crossed, 1 - part, part)
    if halved(share):
        row = lax.div(row, share // 2) * share + part * (share // 2) + lax.rem(row, share // 2)
    else:
        row = part * half + row
    picked_ref[...] = jnp.where(row == slot, 1.0, 0.0).astype(BF16)

    requests, _, key_slots = bias_ref.shape
    key_index = lax.broadcasted_iota(jnp.int32, (new_slots, key_slots), 1)
    query_index = lax.broadcasted_iota(jnp.int32, (new_slots, key_slots), 0)
    is_cache = key_index < cached
    for j in range(requests):
        length, count = lengths_ref[0, j], counts_ref[0, j]
        position = jnp.where(is_cache, key_index, length + key_index - cached)
        relative = position - (length + query_index)
        live = jnp.where(is_cache, key_index - length, key_index - cached - count) < 0
        for h in range(table_ref.shape[0]):
            bias = jnp.where(live, bias_of(table_ref, relative, h), -1e30)
            bias_ref[j, h * new_slots : (h + 1) * new_slots] = bias


def heads_of(shape, heads):
    return lax.broadcasted_iota(jnp.int32, shape, 1) // (shape[1] // heads)


def scores_of(query, keys, bias):
    heads = bias.shape[0] // query.shape[0]
    lane_head = heads_of(query.shape, heads)
    stacked = jnp.concatenate(
        [jnp.where(lane_head == h, query, jnp.zeros_like(query)) for h in range(heads)], axis=0
    )
    scores = lax.dot_general(stacked, keys, (((1,), (1,)), ((), ())), preferred_element_type=F32)
    return scores + bias


def context_of(scores, values, new_slots):
    weights = jnp.exp(scores - jnp.max(scores, axis=1, keepdims=True))
    mixed = dot(weights.astype(BF16), values) / jnp.sum(weights, axis=1, keepdims=True)
    heads = scores.shape[0] // new_slots
    context = mixed[:new_slots]
    lane_head = heads_of(context.shape, heads)
    for h in range(1, heads):
        context = jnp.where(lane_head == h, mixed[h * new_slots : (h + 1) * new_slots], context)
    return context.astype(BF16)


def attend_kernel(
    own_ref,
    far_ref,
    near_ref,
    across_ref,
    gain_ref,
    w_query_ref,
    w_key_ref,
    w_value_ref,
    cache_keys_ref,
    cache_values_ref,
    bias_ref,
    picked_ref,
    send_ref,
    context_ref,
    normed_ref,
):
    index, _ = place()
    rows, width = own_ref.shape
    model_width = gain_ref.shape[1]
    requests = bias_ref.shape[0]
    new_slots, half = rows // requests, rows // 2
    blocks = [(own_ref, 0), (near_ref, 1), (far_ref, 3), (across_ref, 2)]
    squares = 0.0
    for ref, _ in blocks:
        block = ref[...].astype(F32)
        squares = squares + jnp.sum(block * block, axis=1, keepdims=True)
    inverse = lax.rsqrt(squares / model_width + EPSILON)
    for ref, xor in blocks:
        columns = columns_of(index ^ xor, width)
        normed = ref[...].astype(F32) * inverse * gain_ref[:, columns]
        normed_ref[:, columns] = normed.astype(BF16)
    queries = dot(normed_ref[...], w_query_ref[...]).astype(BF16)
    new_keys = dot(normed_ref[...], w_key_ref[...]).astype(BF16)
    scores = []
    for j in range(requests):
        own = slice(j * new_slots, (j + 1) * new_slots)
        keys = jnp.concatenate([cache_keys_ref[j], new_keys[own]], axis=0)
        scores.append(scores_of(queries[own], keys, bias_ref[j]))
    new_values = dot(normed_ref[...], w_value_ref[...]).astype(BF16)
    contexts = []
    for j in range(requests):
        own = slice(j * new_slots, (j + 1) * new_slots)
        values = jnp.concatenate([cache_values_ref[j], new_values[own]], axis=0)
        contexts.append(context_of(scores[j], values, new_slots))
    context = jnp.concatenate(contexts, axis=0)
    context_ref[...] = context
    send_ref[...] = dot(picked_ref[half:], context).astype(BF16)


def project_kernel(context_ref, picked_ref, w_out_ref, keep_ref):
    dealt = dot(picked_ref[: keep_ref.shape[0]], context_ref[...]).astype(BF16)
    keep_ref[...] = dot(dealt, w_out_ref[...])


def pair_kernel(keep_ref, near_ref, near_out_ref, near_inner_ref, *pair_refs):
    del near_inner_ref
    pair = (keep_ref[...] + dot(near_ref[...], near_out_ref[...])).astype(BF16)
    start = 0
    for ref in pair_refs:
        ref[...] = pair[start : start + ref.shape[0]]
        start += ref.shape[0]


def stream_kernel(own_ref, far_ref, near_ref, across_ref, picked_ref, stream_ref):
    index, _ = place()
    width = own_ref.shape[1]
    picked = picked_ref[: stream_ref.shape[0]]
    for ref, xor in ((own_ref, 0), (near_ref, 1), (far_ref, 3), (across_ref, 2)):
        stream_ref[:, columns_of(index ^ xor, width)] = dot(picked, ref[...]).astype(BF16)


def inner_kernel(stream_ref, gain_ref, w_inner_ref, *refs):
    *sum_refs, mixed_ref, input_ref, inverse_ref, hidden_ref = refs
    pieces = len(sum_refs) // 2
    pair = jnp.concatenate([ref[...].astype(F32) for ref in sum_refs[:pieces]], axis=0)
    other = jnp.concatenate([ref[...].astype(F32) for ref in sum_refs[pieces:]], axis=0)
    mixed = pair + other + stream_ref[...].astype(F32)
    mixed_ref[...] = mixed
    square = jnp.sum(mixed * mixed, axis=1, keepdims=True)
    inverse = lax.rsqrt(square / mixed.shape[1] + EPSILON)
    inverse_ref[...] = jnp.broadcast_to(inverse, inverse_ref.shape)
    scaled = (mixed * gain_ref[...]).astype(BF16)
    input_ref[...] = scaled
    hidden_ref[...] = jnp.maximum(dot(scaled, w_inner_ref[...]) * inverse, 0.0).astype(BF16)


def outer_kernel(
    mixed_ref,
    input_ref,
    inverse_ref,
    own_hidden_ref,
    near_inner_ref,
    own_outer_ref,
    near_outer_ref,
    out_ref,
):
    upper = lax.axis_index("hi")
    width = out_ref.shape[2]
    hidden = dot(input_ref[...], near_inner_ref[...]) * inverse_ref[:, :1]
    hidden = jnp.maximum(hidden, 0.0).astype(BF16)
    for t in range(out_ref.shape[0]):
        columns = slice(t * width, (t + 1) * width)
        value = dot(own_hidden_ref[...], own_outer_ref[:, columns])
        value = value + dot(hidden, near_outer_ref[:, columns])
        value = value + jnp.where(upper == t // 2, mixed_ref[:, columns], 0.0)
        out_ref[t] = value.astype(BF16)


def merge_kernel(parts_ref, out_ref):
    replicas, share, _ = out_ref.shape
    crossed = (lax.axis_index("rep") >= straight(replicas, share)).astype(jnp.int32)
    halves = [
        parts_ref[0, lower] + parts_ref[1, lower ^ crossed]
        for lower in range(2)
    ]
    out_ref[...] = jnp.concatenate(halves, axis=1).astype(BF16)


def swap(value, xor):
    return lax.ppermute(value, ("hi", "lo"), [(i, i ^ xor) for i in range(4)])


def on_device(
    replicas,
    tokens,
    attn_gain,
    ffn_gain,
    w_query,
    w_key,
    w_value,
    w_out,
    w_inner,
    w_outer,
    bias_table,
    cache_keys,
    cache_values,
    new_counts,
    cached_lengths,
    deal,
):
    rows, width = tokens.shape
    requests, cached, local_width = cache_keys.shape
    new_slots = rows // requests
    model_width = attn_gain.shape[0]
    head_count = bias_table.shape[1]
    groups = lax.axis_size("hi")
    _, side = place()
    shape = jax.ShapeDtypeStruct
    local = functools.partial(
        pl.pallas_call, compiler_params=pltpu.CompilerParams(vmem_limit_bytes=VMEM_LIMIT)
    )
    across, far = swap(tokens, 2), swap(tokens, 3)
    bias, picked = local(
        functools.partial(prepare_kernel, replicas, cached),
        out_shape=(
            shape((requests, head_count * new_slots, cached + new_slots), F32),
            shape((rows, rows), BF16),
        ),
        in_specs=[SMEM] * 3 + [VMEM],
        out_specs=(VMEM,) * 2,
        cost_estimate=pl.CostEstimate(flops=PREPARE_FLOPS, bytes_accessed=0, transcendentals=0),
        name="prepare",
    )(bias_table.T, new_counts.T, cached_lengths.T, deal)
    blocks = (tokens, far, swap(tokens, 1), across)
    half = rows // 2
    send, context = local(
        attend_kernel,
        out_shape=(shape((half, local_width), BF16), shape((rows, local_width), BF16)),
        in_specs=[VMEM] * 12,
        out_specs=(VMEM,) * 2,
        scratch_shapes=[pltpu.VMEM((rows, model_width), BF16)],
        cost_estimate=pl.CostEstimate(flops=INNER_FLOPS, bytes_accessed=0, transcendentals=0),
        name="attend",
    )(
        *blocks,
        attn_gain.reshape(1, model_width),
        w_query,
        w_key,
        w_value,
        cache_keys,
        cache_values,
        bias,
        picked,
    )
    keep = local(
        project_kernel,
        out_shape=shape((half, model_width), F32),
        in_specs=[VMEM] * 3,
        out_specs=VMEM,
        name="project",
    )(context, picked, w_out)
    stream = local(
        stream_kernel,
        out_shape=shape((half, model_width), BF16),
        in_specs=[VMEM] * 5,
        out_specs=VMEM,
        name="stream",
    )(*blocks, picked)
    share = rows // replicas
    cut = straight(replicas, share) * half // replicas
    sizes = (cut, half - cut) if cut < half else (half,)
    near_inner = swap(w_inner, 1)
    pair = local(
        pair_kernel,
        out_shape=tuple(shape((size, model_width), BF16) for size in sizes),
        in_specs=[VMEM] * 4,
        out_specs=(VMEM,) * len(sizes),
        name="pair",
    )(keep, swap(send, 1), swap(w_out, 1), near_inner)
    late_outer, *pair = lax.optimization_barrier((w_outer, *pair))
    others = [swap(piece, xor) for piece, xor in zip(pair, (2, 3))]
    ff_width = w_inner.shape[1]
    mixed, ffn_input, inverse, hidden = local(
        inner_kernel,
        out_shape=(
            shape((half, model_width), F32),
            shape((half, model_width), BF16),
            shape((half, LANES), F32),
            shape((half, ff_width), BF16),
        ),
        in_specs=[VMEM] * (3 + 2 * len(sizes)),
        out_specs=(VMEM,) * 4,
        cost_estimate=pl.CostEstimate(flops=INNER_FLOPS, bytes_accessed=0, transcendentals=0),
        name="inner",
    )(stream, ffn_gain.reshape(1, model_width), w_inner, *pair, *others)
    out = local(
        outer_kernel,
        out_shape=shape((groups * 2, half, width), BF16),
        in_specs=[VMEM] * 7,
        out_specs=VMEM,
        name="outer",
    )(mixed, ffn_input, inverse, hidden, near_inner, w_outer, swap(late_outer, 1))
    if not halved(share):
        padded = jnp.zeros((groups * 2, rows, width), BF16)
        out = lax.dynamic_update_slice_in_dim(padded, out, side * half, 1)
    parts = lax.all_to_all(
        out.reshape(groups * 2 * replicas, -1, width), ("hi", "lo", "rep"), 0, 0, tiled=True
    )
    parts = parts.reshape(groups, 2, replicas, -1, width).astype(F32)
    if halved(share):
        merged = local(
            merge_kernel,
            out_shape=shape((replicas, share, width), BF16),
            in_specs=[VMEM],
            out_specs=VMEM,
            name="merge",
        )(parts)
        return merged.reshape(rows, width)
    return jnp.sum(parts, axis=(0, 1)).reshape(rows, width).astype(BF16)


def solution(mesh):
    replicas, tp = mesh.shape["rep"], mesh.shape["tp"]
    split = Mesh(mesh.devices.reshape(replicas, tp // 2, 2), ("rep", "hi", "lo"))
    cols = ("hi", "lo")
    in_specs = (
        P("rep", cols),
        P(),
        P(),
        P(None, cols),
        P(None, cols),
        P(None, cols),
        P(cols, None),
        P(None, cols),
        P(cols, None),
        P(None, cols),
        P("rep", None, cols),
        P("rep", None, cols),
        P(None, "rep"),
        P(None, "rep"),
        P("rep", None),
    )
    return jax.shard_map(
        functools.partial(on_device, replicas),
        mesh=split,
        in_specs=in_specs,
        out_specs=P("rep", cols),
        check_vma=False,
    )
```

```python
import functools

import jax
import jax.numpy as jnp
from jax import lax
from jax.experimental import pallas as pl
from jax.experimental.pallas import tpu as pltpu
from jax.sharding import Mesh, PartitionSpec as P

EPSILON = 1e-06
THRESHOLDS = (1, 2, 3, 4, 5, 6, 7, 8, 12, 16, 23, 32, 46, 64, 91)
BF16 = jnp.bfloat16
F32 = jnp.float32
VMEM = pl.BlockSpec(memory_space=pltpu.VMEM)
SMEM = pl.BlockSpec(memory_space=pltpu.SMEM)
PREPARE_FLOPS = 7 * 10**9
INNER_FLOPS = 40 * 10**9
LANES = 128
VMEM_LIMIT = 24 * 1024 * 1024


def dot(a, b):
    return jnp.dot(a, b, preferred_element_type=F32)


def place():
    upper, lower = lax.axis_index("hi"), lax.axis_index("lo")
    return upper * 2 + lower, lower


def straight(replicas, share):
    return replicas * 3 // 4 if halved(share) and replicas % 4 == 0 else replicas


def halved(share):
    return share % 2 == 0


def columns_of(index, width):
    return pl.ds(pl.multiple_of(index * width, width), width)


def bias_of(table_ref, relative, head):
    distance = jnp.abs(relative)
    before = jnp.full(relative.shape, table_ref[head, 0], F32)
    after = jnp.full(relative.shape, table_ref[head, 17], F32)
    for step, threshold in enumerate(THRESHOLDS):
        far = distance >= threshold
        before = jnp.where(far, table_ref[head, step + 1], before)
        after = jnp.where(far, table_ref[head, step + 17], after)
    return jnp.where(relative > 0, after, before)


def prepare_kernel(
    replicas, cached, table_ref, counts_ref, lengths_ref, deal_ref, bias_ref, picked_ref
):
    _, side = place()
    rows = deal_ref.shape[1]
    new_slots = rows // 2
    half, share = rows // 2, rows // replicas
    deal = deal_ref[...]
    slot = lax.rem(deal, replicas) * share + lax.div(deal, replicas)
    lane = lax.broadcasted_iota(jnp.int32, (1, rows), 1)
    live = lane < jnp.where(
        lane < new_slots, counts_ref[0, 0], jnp.minimum(counts_ref[0, 1], new_slots) + new_slots
    )
    slot = jnp.where(live, slot, -1)
    row = lax.broadcasted_iota(jnp.int32, (rows, rows), 0)
    part = jnp.where(row < half, side, 1 - side)
    row = jnp.where(row < half, row, row - half)
    crossed = row >= jnp.where(lax.axis_index("hi") == 0, half, straight(replicas, share) * half // replicas)
    part = jnp.where(crossed, 1 - part, part)
    if halved(share):
        row = lax.div(row, share // 2) * share + part * (share // 2) + lax.rem(row, share // 2)
    else:
        row = part * half + row
    picked_ref[...] = jnp.where(row == slot, 1.0, 0.0).astype(BF16)

    requests, _, key_slots = bias_ref.shape
    key_index = lax.broadcasted_iota(jnp.int32, (new_slots, key_slots), 1)
    query_index = lax.broadcasted_iota(jnp.int32, (new_slots, key_slots), 0)
    is_cache = key_index < cached
    for j in range(requests):
        length, count = lengths_ref[0, j], counts_ref[0, j]
        position = jnp.where(is_cache, key_index, length + key_index - cached)
        relative = position - (length + query_index)
        live = jnp.where(is_cache, key_index - length, key_index - cached - count) < 0
        for h in range(table_ref.shape[0]):
            bias = jnp.where(live, bias_of(table_ref, relative, h), -1e30)
            bias_ref[j, h * new_slots : (h + 1) * new_slots] = bias


def heads_of(shape, heads):
    return lax.broadcasted_iota(jnp.int32, shape, 1) // (shape[1] // heads)


def scores_of(query, keys, bias):
    heads = bias.shape[0] // query.shape[0]
    lane_head = heads_of(query.shape, heads)
    stacked = jnp.concatenate(
        [jnp.where(lane_head == h, query, jnp.zeros_like(query)) for h in range(heads)], axis=0
    )
    scores = lax.dot_general(stacked, keys, (((1,), (1,)), ((), ())), preferred_element_type=F32)
    return scores + bias


def context_of(scores, values, new_slots):
    weights = jnp.exp(scores - jnp.max(scores, axis=1, keepdims=True))
    mixed = dot(weights.astype(BF16), values) / jnp.sum(weights, axis=1, keepdims=True)
    heads = scores.shape[0] // new_slots
    context = mixed[:new_slots]
    lane_head = heads_of(context.shape, heads)
    for h in range(1, heads):
        context = jnp.where(lane_head == h, mixed[h * new_slots : (h + 1) * new_slots], context)
    return context.astype(BF16)


def attend_kernel(
    own_ref,
    far_ref,
    near_ref,
    across_ref,
    gain_ref,
    w_query_ref,
    w_key_ref,
    w_value_ref,
    cache_keys_ref,
    cache_values_ref,
    bias_ref,
    picked_ref,
    send_ref,
    context_ref,
    normed_ref,
):
    index, _ = place()
    rows, width = own_ref.shape
    model_width = gain_ref.shape[1]
    requests = bias_ref.shape[0]
    new_slots, half = rows // requests, rows // 2
    blocks = [(own_ref, 0), (near_ref, 1), (far_ref, 3), (across_ref, 2)]
    squares = 0.0
    for ref, _ in blocks:
        block = ref[...].astype(F32)
        squares = squares + jnp.sum(block * block, axis=1, keepdims=True)
    inverse = lax.rsqrt(squares / model_width + EPSILON)
    for ref, xor in blocks:
        columns = columns_of(index ^ xor, width)
        normed = ref[...].astype(F32) * inverse * gain_ref[:, columns]
        normed_ref[:, columns] = normed.astype(BF16)
    queries = dot(normed_ref[...], w_query_ref[...]).astype(BF16)
    new_keys = dot(normed_ref[...], w_key_ref[...]).astype(BF16)
    scores = []
    for j in range(requests):
        own = slice(j * new_slots, (j + 1) * new_slots)
        keys = jnp.concatenate([cache_keys_ref[j], new_keys[own]], axis=0)
        scores.append(scores_of(queries[own], keys, bias_ref[j]))
    new_values = dot(normed_ref[...], w_value_ref[...]).astype(BF16)
    contexts = []
    for j in range(requests):
        own = slice(j * new_slots, (j + 1) * new_slots)
        values = jnp.concatenate([cache_values_ref[j], new_values[own]], axis=0)
        contexts.append(context_of(scores[j], values, new_slots))
    context = jnp.concatenate(contexts, axis=0)
    context_ref[...] = context
    send_ref[...] = dot(picked_ref[half:], context).astype(BF16)


def project_kernel(context_ref, picked_ref, w_out_ref, keep_ref):
    dealt = dot(picked_ref[: keep_ref.shape[0]], context_ref[...]).astype(BF16)
    keep_ref[...] = dot(dealt, w_out_ref[...])


def pair_kernel(keep_ref, near_ref, near_out_ref, near_inner_ref, near_outer_ref, *pair_refs):
    del near_inner_ref, near_outer_ref
    pair = (keep_ref[...] + dot(near_ref[...], near_out_ref[...])).astype(BF16)
    start = 0
    for ref in pair_refs:
        ref[...] = pair[start : start + ref.shape[0]]
        start += ref.shape[0]


def stream_kernel(own_ref, far_ref, near_ref, across_ref, picked_ref, stream_ref):
    index, _ = place()
    width = own_ref.shape[1]
    picked = picked_ref[: stream_ref.shape[0]]
    for ref, xor in ((own_ref, 0), (near_ref, 1), (far_ref, 3), (across_ref, 2)):
        stream_ref[:, columns_of(index ^ xor, width)] = dot(picked, ref[...]).astype(BF16)


def ffn_kernel(
    stream_ref, gain_ref, own_inner_ref, near_inner_ref, own_outer_ref, near_outer_ref, *refs
):
    *sum_refs, out_ref = refs
    pieces = len(sum_refs) // 2
    pair = jnp.concatenate([ref[...].astype(F32) for ref in sum_refs[:pieces]], axis=0)
    other = jnp.concatenate([ref[...].astype(F32) for ref in sum_refs[pieces:]], axis=0)
    mixed = pair + other + stream_ref[...].astype(F32)
    square = jnp.sum(mixed * mixed, axis=1, keepdims=True)
    inverse = lax.rsqrt(square / mixed.shape[1] + EPSILON)
    scaled = (mixed * gain_ref[...]).astype(BF16)
    own, near = (
        jnp.maximum(dot(scaled, ref[...]) * inverse, 0.0).astype(BF16)
        for ref in (own_inner_ref, near_inner_ref)
    )
    upper = lax.axis_index("hi")
    width = out_ref.shape[2]
    for t in range(out_ref.shape[0]):
        columns = slice(t * width, (t + 1) * width)
        value = dot(own, own_outer_ref[:, columns]) + dot(near, near_outer_ref[:, columns])
        value = value + jnp.where(upper == t // 2, mixed[:, columns], 0.0)
        out_ref[t] = value.astype(BF16)


def merge_kernel(parts_ref, out_ref):
    replicas, share, _ = out_ref.shape
    crossed = (lax.axis_index("rep") >= straight(replicas, share)).astype(jnp.int32)
    halves = [
        parts_ref[0, lower] + parts_ref[1, lower ^ crossed]
        for lower in range(2)
    ]
    out_ref[...] = jnp.concatenate(halves, axis=1).astype(BF16)


def swap(value, xor):
    return lax.ppermute(value, ("hi", "lo"), [(i, i ^ xor) for i in range(4)])


def on_device(
    replicas,
    tokens,
    attn_gain,
    ffn_gain,
    w_query,
    w_key,
    w_value,
    w_out,
    w_inner,
    w_outer,
    bias_table,
    cache_keys,
    cache_values,
    new_counts,
    cached_lengths,
    deal,
):
    rows, width = tokens.shape
    requests, cached, local_width = cache_keys.shape
    new_slots = rows // requests
    model_width = attn_gain.shape[0]
    head_count = bias_table.shape[1]
    groups = lax.axis_size("hi")
    _, side = place()
    shape = jax.ShapeDtypeStruct
    local = functools.partial(
        pl.pallas_call, compiler_params=pltpu.CompilerParams(vmem_limit_bytes=VMEM_LIMIT)
    )
    across, far = swap(tokens, 2), swap(tokens, 3)
    bias, picked = local(
        functools.partial(prepare_kernel, replicas, cached),
        out_shape=(
            shape((requests, head_count * new_slots, cached + new_slots), F32),
            shape((rows, rows), BF16),
        ),
        in_specs=[SMEM] * 3 + [VMEM],
        out_specs=(VMEM,) * 2,
        cost_estimate=pl.CostEstimate(flops=PREPARE_FLOPS, bytes_accessed=0, transcendentals=0),
        name="prepare",
    )(bias_table.T, new_counts.T, cached_lengths.T, deal)
    blocks = (tokens, far, swap(tokens, 1), across)
    half = rows // 2
    send, context = local(
        attend_kernel,
        out_shape=(shape((half, local_width), BF16), shape((rows, local_width), BF16)),
        in_specs=[VMEM] * 12,
        out_specs=(VMEM,) * 2,
        scratch_shapes=[pltpu.VMEM((rows, model_width), BF16)],
        cost_estimate=pl.CostEstimate(flops=INNER_FLOPS, bytes_accessed=0, transcendentals=0),
        name="attend",
    )(
        *blocks,
        attn_gain.reshape(1, model_width),
        w_query,
        w_key,
        w_value,
        cache_keys,
        cache_values,
        bias,
        picked,
    )
    keep = local(
        project_kernel,
        out_shape=shape((half, model_width), F32),
        in_specs=[VMEM] * 3,
        out_specs=VMEM,
        name="project",
    )(context, picked, w_out)
    stream = local(
        stream_kernel,
        out_shape=shape((half, model_width), BF16),
        in_specs=[VMEM] * 5,
        out_specs=VMEM,
        name="stream",
    )(*blocks, picked)
    share = rows // replicas
    cut = straight(replicas, share) * half // replicas
    sizes = (cut, half - cut) if cut < half else (half,)
    near_inner, near_outer = swap(w_inner, 1), swap(w_outer, 1)
    pair = local(
        pair_kernel,
        out_shape=tuple(shape((size, model_width), BF16) for size in sizes),
        in_specs=[VMEM] * 5,
        out_specs=(VMEM,) * len(sizes),
        name="pair",
    )(keep, swap(send, 1), swap(w_out, 1), near_inner, near_outer)
    others = [swap(piece, xor) for piece, xor in zip(pair, (2, 3))]
    out = local(
        ffn_kernel,
        out_shape=shape((groups * 2, half, width), BF16),
        in_specs=[VMEM] * (6 + 2 * len(sizes)),
        out_specs=VMEM,
        name="ffn",
    )(
        stream,
        ffn_gain.reshape(1, model_width),
        w_inner,
        near_inner,
        w_outer,
        near_outer,
        *pair,
        *others,
    )
    if not halved(share):
        padded = jnp.zeros((groups * 2, rows, width), BF16)
        out = lax.dynamic_update_slice_in_dim(padded, out, side * half, 1)
    parts = lax.all_to_all(
        out.reshape(groups * 2 * replicas, -1, width), ("hi", "lo", "rep"), 0, 0, tiled=True
    )
    parts = parts.reshape(groups, 2, replicas, -1, width).astype(F32)
    if halved(share):
        merged = local(
            merge_kernel,
            out_shape=shape((replicas, share, width), BF16),
            in_specs=[VMEM],
            out_specs=VMEM,
            name="merge",
        )(parts)
        return merged.reshape(rows, width)
    return jnp.sum(parts, axis=(0, 1)).reshape(rows, width).astype(BF16)


def solution(mesh):
    replicas, tp = mesh.shape["rep"], mesh.shape["tp"]
    split = Mesh(mesh.devices.reshape(replicas, tp // 2, 2), ("rep", "hi", "lo"))
    cols = ("hi", "lo")
    in_specs = (
        P("rep", cols),
        P(),
        P(),
        P(None, cols),
        P(None, cols),
        P(None, cols),
        P(cols, None),
        P(None, cols),
        P(cols, None),
        P(None, cols),
        P("rep", None, cols),
        P("rep", None, cols),
        P(None, "rep"),
        P(None, "rep"),
        P("rep", None),
    )
    return jax.shard_map(
        functools.partial(on_device, replicas),
        mesh=split,
        in_specs=in_specs,
        out_specs=P("rep", cols),
        check_vma=False,
    )
```

```python
import functools

import jax
import jax.numpy as jnp
from jax import lax
from jax.experimental import pallas as pl
from jax.experimental.pallas import tpu as pltpu
from jax.sharding import Mesh, PartitionSpec as P

EPSILON = 1e-06
THRESHOLDS = (1, 2, 3, 4, 5, 6, 7, 8, 12, 16, 23, 32, 46, 64, 91)
BF16 = jnp.bfloat16
F32 = jnp.float32
VMEM = pl.BlockSpec(memory_space=pltpu.VMEM)
SMEM = pl.BlockSpec(memory_space=pltpu.SMEM)
PREPARE_FLOPS = 7 * 10**9
INNER_FLOPS = 40 * 10**9
LANES = 128
VMEM_LIMIT = 24 * 1024 * 1024


def dot(a, b):
    return jnp.dot(a, b, preferred_element_type=F32)


def place():
    upper, lower = lax.axis_index("hi"), lax.axis_index("lo")
    return upper * 2 + lower, lower


def straight(replicas, share):
    return replicas // 2 if halved(share) and replicas % 4 == 0 else replicas


def halved(share):
    return share % 2 == 0


def columns_of(index, width):
    return pl.ds(pl.multiple_of(index * width, width), width)


def bias_of(table_ref, relative, head):
    distance = jnp.abs(relative)
    before = jnp.full(relative.shape, table_ref[head, 0], F32)
    after = jnp.full(relative.shape, table_ref[head, 17], F32)
    for step, threshold in enumerate(THRESHOLDS):
        far = distance >= threshold
        before = jnp.where(far, table_ref[head, step + 1], before)
        after = jnp.where(far, table_ref[head, step + 17], after)
    return jnp.where(relative > 0, after, before)


def prepare_kernel(
    replicas, cached, table_ref, counts_ref, lengths_ref, deal_ref, bias_ref, picked_ref
):
    _, side = place()
    rows = deal_ref.shape[1]
    new_slots = rows // 2
    half, share = rows // 2, rows // replicas
    deal = deal_ref[...]
    slot = lax.rem(deal, replicas) * share + lax.div(deal, replicas)
    lane = lax.broadcasted_iota(jnp.int32, (1, rows), 1)
    live = lane < jnp.where(
        lane < new_slots, counts_ref[0, 0], jnp.minimum(counts_ref[0, 1], new_slots) + new_slots
    )
    slot = jnp.where(live, slot, -1)
    row = lax.broadcasted_iota(jnp.int32, (rows, rows), 0)
    part = jnp.where(row < half, side, 1 - side)
    row = jnp.where(row < half, row, row - half)
    crossed = row >= jnp.where(lax.axis_index("hi") == 0, half, straight(replicas, share) * half // replicas)
    part = jnp.where(crossed, 1 - part, part)
    if halved(share):
        row = lax.div(row, share // 2) * share + part * (share // 2) + lax.rem(row, share // 2)
    else:
        row = part * half + row
    picked_ref[...] = jnp.where(row == slot, 1.0, 0.0).astype(BF16)

    requests, _, key_slots = bias_ref.shape
    key_index = lax.broadcasted_iota(jnp.int32, (new_slots, key_slots), 1)
    query_index = lax.broadcasted_iota(jnp.int32, (new_slots, key_slots), 0)
    is_cache = key_index < cached
    for j in range(requests):
        length, count = lengths_ref[0, j], counts_ref[0, j]
        position = jnp.where(is_cache, key_index, length + key_index - cached)
        relative = position - (length + query_index)
        live = jnp.where(is_cache, key_index - length, key_index - cached - count) < 0
        for h in range(table_ref.shape[0]):
            bias = jnp.where(live, bias_of(table_ref, relative, h), -1e30)
            bias_ref[j, h * new_slots : (h + 1) * new_slots] = bias


def heads_of(shape, heads):
    return lax.broadcasted_iota(jnp.int32, shape, 1) // (shape[1] // heads)


def scores_of(query, keys, bias):
    heads = bias.shape[0] // query.shape[0]
    lane_head = heads_of(query.shape, heads)
    stacked = jnp.concatenate(
        [jnp.where(lane_head == h, query, jnp.zeros_like(query)) for h in range(heads)], axis=0
    )
    scores = lax.dot_general(stacked, keys, (((1,), (1,)), ((), ())), preferred_element_type=F32)
    return scores + bias


def context_of(scores, values, new_slots):
    weights = jnp.exp(scores - jnp.max(scores, axis=1, keepdims=True))
    mixed = dot(weights.astype(BF16), values) / jnp.sum(weights, axis=1, keepdims=True)
    heads = scores.shape[0] // new_slots
    context = mixed[:new_slots]
    lane_head = heads_of(context.shape, heads)
    for h in range(1, heads):
        context = jnp.where(lane_head == h, mixed[h * new_slots : (h + 1) * new_slots], context)
    return context.astype(BF16)


def attend_kernel(
    own_ref,
    far_ref,
    near_ref,
    across_ref,
    gain_ref,
    w_query_ref,
    w_key_ref,
    w_value_ref,
    cache_keys_ref,
    cache_values_ref,
    bias_ref,
    picked_ref,
    send_ref,
    context_ref,
    normed_ref,
):
    index, _ = place()
    rows, width = own_ref.shape
    model_width = gain_ref.shape[1]
    requests = bias_ref.shape[0]
    new_slots, half = rows // requests, rows // 2
    blocks = [(own_ref, 0), (near_ref, 1), (far_ref, 3), (across_ref, 2)]
    squares = 0.0
    for ref, _ in blocks:
        block = ref[...].astype(F32)
        squares = squares + jnp.sum(block * block, axis=1, keepdims=True)
    inverse = lax.rsqrt(squares / model_width + EPSILON)
    for ref, xor in blocks:
        columns = columns_of(index ^ xor, width)
        normed = ref[...].astype(F32) * inverse * gain_ref[:, columns]
        normed_ref[:, columns] = normed.astype(BF16)
    queries = dot(normed_ref[...], w_query_ref[...]).astype(BF16)
    new_keys = dot(normed_ref[...], w_key_ref[...]).astype(BF16)
    scores = []
    for j in range(requests):
        own = slice(j * new_slots, (j + 1) * new_slots)
        keys = jnp.concatenate([cache_keys_ref[j], new_keys[own]], axis=0)
        scores.append(scores_of(queries[own], keys, bias_ref[j]))
    new_values = dot(normed_ref[...], w_value_ref[...]).astype(BF16)
    contexts = []
    for j in range(requests):
        own = slice(j * new_slots, (j + 1) * new_slots)
        values = jnp.concatenate([cache_values_ref[j], new_values[own]], axis=0)
        contexts.append(context_of(scores[j], values, new_slots))
    context = jnp.concatenate(contexts, axis=0)
    context_ref[...] = context
    send_ref[...] = dot(picked_ref[half:], context).astype(BF16)


def project_kernel(context_ref, picked_ref, w_out_ref, keep_ref):
    dealt = dot(picked_ref[: keep_ref.shape[0]], context_ref[...]).astype(BF16)
    keep_ref[...] = dot(dealt, w_out_ref[...])


def pair_kernel(keep_ref, near_ref, near_out_ref, near_inner_ref, near_outer_ref, *pair_refs):
    del near_inner_ref, near_outer_ref
    pair = (keep_ref[...] + dot(near_ref[...], near_out_ref[...])).astype(BF16)
    start = 0
    for ref in pair_refs:
        ref[...] = pair[start : start + ref.shape[0]]
        start += ref.shape[0]


def stream_kernel(own_ref, far_ref, near_ref, across_ref, picked_ref, stream_ref):
    index, _ = place()
    width = own_ref.shape[1]
    picked = picked_ref[: stream_ref.shape[0]]
    for ref, xor in ((own_ref, 0), (near_ref, 1), (far_ref, 3), (across_ref, 2)):
        stream_ref[:, columns_of(index ^ xor, width)] = dot(picked, ref[...]).astype(BF16)


def ffn_kernel(
    stream_ref, gain_ref, own_inner_ref, near_inner_ref, own_outer_ref, near_outer_ref, *refs
):
    *sum_refs, out_ref = refs
    pieces = len(sum_refs) // 2
    pair = jnp.concatenate([ref[...].astype(F32) for ref in sum_refs[:pieces]], axis=0)
    other = jnp.concatenate([ref[...].astype(F32) for ref in sum_refs[pieces:]], axis=0)
    mixed = pair + other + stream_ref[...].astype(F32)
    square = jnp.sum(mixed * mixed, axis=1, keepdims=True)
    inverse = lax.rsqrt(square / mixed.shape[1] + EPSILON)
    scaled = (mixed * gain_ref[...]).astype(BF16)
    own, near = (
        jnp.maximum(dot(scaled, ref[...]) * inverse, 0.0).astype(BF16)
        for ref in (own_inner_ref, near_inner_ref)
    )
    upper = lax.axis_index("hi")
    width = out_ref.shape[2]
    for t in range(out_ref.shape[0]):
        columns = slice(t * width, (t + 1) * width)
        value = dot(own, own_outer_ref[:, columns]) + dot(near, near_outer_ref[:, columns])
        value = value + jnp.where(upper == t // 2, mixed[:, columns], 0.0)
        out_ref[t] = value.astype(BF16)


def merge_kernel(parts_ref, out_ref):
    replicas, share, _ = out_ref.shape
    crossed = (lax.axis_index("rep") >= straight(replicas, share)).astype(jnp.int32)
    halves = [
        parts_ref[0, lower] + parts_ref[1, lower ^ crossed]
        for lower in range(2)
    ]
    out_ref[...] = jnp.concatenate(halves, axis=1).astype(BF16)


def swap(value, xor):
    return lax.ppermute(value, ("hi", "lo"), [(i, i ^ xor) for i in range(4)])


def on_device(
    replicas,
    tokens,
    attn_gain,
    ffn_gain,
    w_query,
    w_key,
    w_value,
    w_out,
    w_inner,
    w_outer,
    bias_table,
    cache_keys,
    cache_values,
    new_counts,
    cached_lengths,
    deal,
):
    rows, width = tokens.shape
    requests, cached, local_width = cache_keys.shape
    new_slots = rows // requests
    model_width = attn_gain.shape[0]
    head_count = bias_table.shape[1]
    groups = lax.axis_size("hi")
    _, side = place()
    shape = jax.ShapeDtypeStruct
    local = functools.partial(
        pl.pallas_call, compiler_params=pltpu.CompilerParams(vmem_limit_bytes=VMEM_LIMIT)
    )
    across, far = swap(tokens, 2), swap(tokens, 3)
    bias, picked = local(
        functools.partial(prepare_kernel, replicas, cached),
        out_shape=(
            shape((requests, head_count * new_slots, cached + new_slots), F32),
            shape((rows, rows), BF16),
        ),
        in_specs=[SMEM] * 3 + [VMEM],
        out_specs=(VMEM,) * 2,
        cost_estimate=pl.CostEstimate(flops=PREPARE_FLOPS, bytes_accessed=0, transcendentals=0),
        name="prepare",
    )(bias_table.T, new_counts.T, cached_lengths.T, deal)
    blocks = (tokens, far, swap(tokens, 1), across)
    half = rows // 2
    send, context = local(
        attend_kernel,
        out_shape=(shape((half, local_width), BF16), shape((rows, local_width), BF16)),
        in_specs=[VMEM] * 12,
        out_specs=(VMEM,) * 2,
        scratch_shapes=[pltpu.VMEM((rows, model_width), BF16)],
        cost_estimate=pl.CostEstimate(flops=INNER_FLOPS, bytes_accessed=0, transcendentals=0),
        name="attend",
    )(
        *blocks,
        attn_gain.reshape(1, model_width),
        w_query,
        w_key,
        w_value,
        cache_keys,
        cache_values,
        bias,
        picked,
    )
    keep = local(
        project_kernel,
        out_shape=shape((half, model_width), F32),
        in_specs=[VMEM] * 3,
        out_specs=VMEM,
        name="project",
    )(context, picked, w_out)
    stream = local(
        stream_kernel,
        out_shape=shape((half, model_width), BF16),
        in_specs=[VMEM] * 5,
        out_specs=VMEM,
        name="stream",
    )(*blocks, picked)
    share = rows // replicas
    cut = straight(replicas, share) * half // replicas
    sizes = (cut, half - cut) if cut < half else (half,)
    near_inner, near_outer = swap(w_inner, 1), swap(w_outer, 1)
    pair = local(
        pair_kernel,
        out_shape=tuple(shape((size, model_width), BF16) for size in sizes),
        in_specs=[VMEM] * 5,
        out_specs=(VMEM,) * len(sizes),
        name="pair",
    )(keep, swap(send, 1), swap(w_out, 1), near_inner, near_outer)
    others = [swap(piece, xor) for piece, xor in zip(pair, (2, 3))]
    out = local(
        ffn_kernel,
        out_shape=shape((groups * 2, half, width), BF16),
        in_specs=[VMEM] * (6 + 2 * len(sizes)),
        out_specs=VMEM,
        name="ffn",
    )(
        stream,
        ffn_gain.reshape(1, model_width),
        w_inner,
        near_inner,
        w_outer,
        near_outer,
        *pair,
        *others,
    )
    if not halved(share):
        padded = jnp.zeros((groups * 2, rows, width), BF16)
        out = lax.dynamic_update_slice_in_dim(padded, out, side * half, 1)
    parts = lax.all_to_all(
        out.reshape(groups * 2 * replicas, -1, width), ("hi", "lo", "rep"), 0, 0, tiled=True
    )
    parts = parts.reshape(groups, 2, replicas, -1, width).astype(F32)
    if halved(share):
        merged = local(
            merge_kernel,
            out_shape=shape((replicas, share, width), BF16),
            in_specs=[VMEM],
            out_specs=VMEM,
            name="merge",
        )(parts)
        return merged.reshape(rows, width)
    return jnp.sum(parts, axis=(0, 1)).reshape(rows, width).astype(BF16)


def solution(mesh):
    replicas, tp = mesh.shape["rep"], mesh.shape["tp"]
    split = Mesh(mesh.devices.reshape(replicas, tp // 2, 2), ("rep", "hi", "lo"))
    cols = ("hi", "lo")
    in_specs = (
        P("rep", cols),
        P(),
        P(),
        P(None, cols),
        P(None, cols),
        P(None, cols),
        P(cols, None),
        P(None, cols),
        P(cols, None),
        P(None, cols),
        P("rep", None, cols),
        P("rep", None, cols),
        P(None, "rep"),
        P(None, "rep"),
        P("rep", None),
    )
    return jax.shard_map(
        functools.partial(on_device, replicas),
        mesh=split,
        in_specs=in_specs,
        out_specs=P("rep", cols),
        check_vma=False,
    )
```

```python
import functools

import jax
import jax.numpy as jnp
from jax import lax
from jax.experimental import pallas as pl
from jax.experimental.pallas import tpu as pltpu
from jax.sharding import Mesh, PartitionSpec as P

EPSILON = 1e-06
THRESHOLDS = (1, 2, 3, 4, 5, 6, 7, 8, 12, 16, 23, 32, 46, 64, 91)
BF16 = jnp.bfloat16
F32 = jnp.float32
VMEM = pl.BlockSpec(memory_space=pltpu.VMEM)
SMEM = pl.BlockSpec(memory_space=pltpu.SMEM)
PREPARE_FLOPS = 7 * 10**9
INNER_FLOPS = 40 * 10**9
LANES = 128
VMEM_LIMIT = 24 * 1024 * 1024


def dot(a, b):
    return jnp.dot(a, b, preferred_element_type=F32)


def place():
    upper, lower = lax.axis_index("hi"), lax.axis_index("lo")
    return upper * 2 + lower, lower


def straight(replicas, share):
    return replicas // 2 if halved(share) and replicas % 4 == 0 else replicas


def halved(share):
    return share % 2 == 0


def columns_of(index, width):
    return pl.ds(pl.multiple_of(index * width, width), width)


def bias_of(table_ref, relative, head):
    distance = jnp.abs(relative)
    before = jnp.full(relative.shape, table_ref[head, 0], F32)
    after = jnp.full(relative.shape, table_ref[head, 17], F32)
    for step, threshold in enumerate(THRESHOLDS):
        far = distance >= threshold
        before = jnp.where(far, table_ref[head, step + 1], before)
        after = jnp.where(far, table_ref[head, step + 17], after)
    return jnp.where(relative > 0, after, before)


def prepare_kernel(
    replicas, cached, table_ref, counts_ref, lengths_ref, deal_ref, bias_ref, picked_ref
):
    _, side = place()
    rows = deal_ref.shape[1]
    new_slots = rows // 2
    half, share = rows // 2, rows // replicas
    deal = deal_ref[...]
    slot = lax.rem(deal, replicas) * share + lax.div(deal, replicas)
    lane = lax.broadcasted_iota(jnp.int32, (1, rows), 1)
    live = lane < jnp.where(
        lane < new_slots, counts_ref[0, 0], jnp.minimum(counts_ref[0, 1], new_slots) + new_slots
    )
    slot = jnp.where(live, slot, -1)
    row = lax.broadcasted_iota(jnp.int32, (rows, rows), 0)
    part = jnp.where(row < half, side, 1 - side)
    row = jnp.where(row < half, row, row - half)
    crossed = row >= jnp.where(lax.axis_index("hi") == 0, half, straight(replicas, share) * half // replicas)
    part = jnp.where(crossed, 1 - part, part)
    if halved(share):
        row = lax.div(row, share // 2) * share + part * (share // 2) + lax.rem(row, share // 2)
    else:
        row = part * half + row
    picked_ref[...] = jnp.where(row == slot, 1.0, 0.0).astype(BF16)

    requests, _, key_slots = bias_ref.shape
    key_index = lax.broadcasted_iota(jnp.int32, (new_slots, key_slots), 1)
    query_index = lax.broadcasted_iota(jnp.int32, (new_slots, key_slots), 0)
    is_cache = key_index < cached
    for j in range(requests):
        length, count = lengths_ref[0, j], counts_ref[0, j]
        position = jnp.where(is_cache, key_index, length + key_index - cached)
        relative = position - (length + query_index)
        live = jnp.where(is_cache, key_index - length, key_index - cached - count) < 0
        for h in range(table_ref.shape[0]):
            bias = jnp.where(live, bias_of(table_ref, relative, h), -1e30)
            bias_ref[j, h * new_slots : (h + 1) * new_slots] = bias


def heads_of(shape, heads):
    return lax.broadcasted_iota(jnp.int32, shape, 1) // (shape[1] // heads)


def scores_of(query, keys, bias):
    heads = bias.shape[0] // query.shape[0]
    lane_head = heads_of(query.shape, heads)
    stacked = jnp.concatenate(
        [jnp.where(lane_head == h, query, jnp.zeros_like(query)) for h in range(heads)], axis=0
    )
    scores = lax.dot_general(stacked, keys, (((1,), (1,)), ((), ())), preferred_element_type=F32)
    return scores + bias


def context_of(scores, values, new_slots):
    weights = jnp.exp(scores - jnp.max(scores, axis=1, keepdims=True))
    mixed = dot(weights.astype(BF16), values) / jnp.sum(weights, axis=1, keepdims=True)
    heads = scores.shape[0] // new_slots
    context = mixed[:new_slots]
    lane_head = heads_of(context.shape, heads)
    for h in range(1, heads):
        context = jnp.where(lane_head == h, mixed[h * new_slots : (h + 1) * new_slots], context)
    return context.astype(BF16)


def attend_kernel(
    own_ref,
    far_ref,
    near_ref,
    across_ref,
    gain_ref,
    w_query_ref,
    w_key_ref,
    w_value_ref,
    cache_keys_ref,
    cache_values_ref,
    bias_ref,
    picked_ref,
    send_ref,
    context_ref,
    normed_ref,
):
    index, _ = place()
    rows, width = own_ref.shape
    model_width = gain_ref.shape[1]
    requests = bias_ref.shape[0]
    new_slots, half = rows // requests, rows // 2
    blocks = [(own_ref, 0), (near_ref, 1), (far_ref, 3), (across_ref, 2)]
    squares = 0.0
    for ref, _ in blocks:
        block = ref[...].astype(F32)
        squares = squares + jnp.sum(block * block, axis=1, keepdims=True)
    inverse = lax.rsqrt(squares / model_width + EPSILON)
    for ref, xor in blocks:
        columns = columns_of(index ^ xor, width)
        normed = ref[...].astype(F32) * inverse * gain_ref[:, columns]
        normed_ref[:, columns] = normed.astype(BF16)
    queries = dot(normed_ref[...], w_query_ref[...]).astype(BF16)
    new_keys = dot(normed_ref[...], w_key_ref[...]).astype(BF16)
    scores = []
    for j in range(requests):
        own = slice(j * new_slots, (j + 1) * new_slots)
        keys = jnp.concatenate([cache_keys_ref[j], new_keys[own]], axis=0)
        scores.append(scores_of(queries[own], keys, bias_ref[j]))
    new_values = dot(normed_ref[...], w_value_ref[...]).astype(BF16)
    contexts = []
    for j in range(requests):
        own = slice(j * new_slots, (j + 1) * new_slots)
        values = jnp.concatenate([cache_values_ref[j], new_values[own]], axis=0)
        contexts.append(context_of(scores[j], values, new_slots))
    context = jnp.concatenate(contexts, axis=0)
    context_ref[...] = context
    send_ref[...] = dot(picked_ref[half:], context).astype(BF16)


def project_kernel(context_ref, picked_ref, w_out_ref, keep_ref):
    dealt = dot(picked_ref[: keep_ref.shape[0]], context_ref[...]).astype(BF16)
    keep_ref[...] = dot(dealt, w_out_ref[...])


def pair_kernel(start, keep_ref, near_ref, near_out_ref, near_inner_ref, near_outer_ref, pair_ref):
    del near_inner_ref, near_outer_ref
    rows = slice(start, start + pair_ref.shape[0])
    pair_ref[...] = (keep_ref[rows] + dot(near_ref[rows], near_out_ref[...])).astype(BF16)


def stream_kernel(own_ref, far_ref, near_ref, across_ref, picked_ref, stream_ref):
    index, _ = place()
    width = own_ref.shape[1]
    picked = picked_ref[: stream_ref.shape[0]]
    for ref, xor in ((own_ref, 0), (near_ref, 1), (far_ref, 3), (across_ref, 2)):
        stream_ref[:, columns_of(index ^ xor, width)] = dot(picked, ref[...]).astype(BF16)


def ffn_kernel(
    stream_ref, gain_ref, own_inner_ref, near_inner_ref, own_outer_ref, near_outer_ref, *refs
):
    *sum_refs, out_ref = refs
    pieces = len(sum_refs) // 2
    pair = jnp.concatenate([ref[...].astype(F32) for ref in sum_refs[:pieces]], axis=0)
    other = jnp.concatenate([ref[...].astype(F32) for ref in sum_refs[pieces:]], axis=0)
    mixed = pair + other + stream_ref[...].astype(F32)
    square = jnp.sum(mixed * mixed, axis=1, keepdims=True)
    inverse = lax.rsqrt(square / mixed.shape[1] + EPSILON)
    scaled = (mixed * gain_ref[...]).astype(BF16)
    own, near = (
        jnp.maximum(dot(scaled, ref[...]) * inverse, 0.0).astype(BF16)
        for ref in (own_inner_ref, near_inner_ref)
    )
    upper = lax.axis_index("hi")
    width = out_ref.shape[2]
    for t in range(out_ref.shape[0]):
        columns = slice(t * width, (t + 1) * width)
        value = dot(own, own_outer_ref[:, columns]) + dot(near, near_outer_ref[:, columns])
        value = value + jnp.where(upper == t // 2, mixed[:, columns], 0.0)
        out_ref[t] = value.astype(BF16)


def merge_kernel(parts_ref, out_ref):
    replicas, share, _ = out_ref.shape
    crossed = (lax.axis_index("rep") >= straight(replicas, share)).astype(jnp.int32)
    halves = [
        parts_ref[0, lower] + parts_ref[1, lower ^ crossed]
        for lower in range(2)
    ]
    out_ref[...] = jnp.concatenate(halves, axis=1).astype(BF16)


def swap(value, xor):
    return lax.ppermute(value, ("hi", "lo"), [(i, i ^ xor) for i in range(4)])


def on_device(
    replicas,
    tokens,
    attn_gain,
    ffn_gain,
    w_query,
    w_key,
    w_value,
    w_out,
    w_inner,
    w_outer,
    bias_table,
    cache_keys,
    cache_values,
    new_counts,
    cached_lengths,
    deal,
):
    rows, width = tokens.shape
    requests, cached, local_width = cache_keys.shape
    new_slots = rows // requests
    model_width = attn_gain.shape[0]
    head_count = bias_table.shape[1]
    groups = lax.axis_size("hi")
    _, side = place()
    shape = jax.ShapeDtypeStruct
    local = functools.partial(
        pl.pallas_call, compiler_params=pltpu.CompilerParams(vmem_limit_bytes=VMEM_LIMIT)
    )
    across, far = swap(tokens, 2), swap(tokens, 3)
    bias, picked = local(
        functools.partial(prepare_kernel, replicas, cached),
        out_shape=(
            shape((requests, head_count * new_slots, cached + new_slots), F32),
            shape((rows, rows), BF16),
        ),
        in_specs=[SMEM] * 3 + [VMEM],
        out_specs=(VMEM,) * 2,
        cost_estimate=pl.CostEstimate(flops=PREPARE_FLOPS, bytes_accessed=0, transcendentals=0),
        name="prepare",
    )(bias_table.T, new_counts.T, cached_lengths.T, deal)
    blocks = (tokens, far, swap(tokens, 1), across)
    half = rows // 2
    send, context = local(
        attend_kernel,
        out_shape=(shape((half, local_width), BF16), shape((rows, local_width), BF16)),
        in_specs=[VMEM] * 12,
        out_specs=(VMEM,) * 2,
        scratch_shapes=[pltpu.VMEM((rows, model_width), BF16)],
        cost_estimate=pl.CostEstimate(flops=INNER_FLOPS, bytes_accessed=0, transcendentals=0),
        name="attend",
    )(
        *blocks,
        attn_gain.reshape(1, model_width),
        w_query,
        w_key,
        w_value,
        cache_keys,
        cache_values,
        bias,
        picked,
    )
    keep = local(
        project_kernel,
        out_shape=shape((half, model_width), F32),
        in_specs=[VMEM] * 3,
        out_specs=VMEM,
        name="project",
    )(context, picked, w_out)
    stream = local(
        stream_kernel,
        out_shape=shape((half, model_width), BF16),
        in_specs=[VMEM] * 5,
        out_specs=VMEM,
        name="stream",
    )(*blocks, picked)
    share = rows // replicas
    cut = straight(replicas, share) * half // replicas
    sizes = (cut, half - cut) if cut < half else (half,)
    near_inner, near_outer = swap(w_inner, 1), swap(w_outer, 1)
    operands = (keep, swap(send, 1), swap(w_out, 1), near_inner, near_outer)
    pair = [
        local(
            functools.partial(pair_kernel, start),
            out_shape=shape((size, model_width), BF16),
            in_specs=[VMEM] * 5,
            out_specs=VMEM,
            name="pair",
        )(*operands)
        for start, size in zip((0, cut), sizes)
    ]
    others = [swap(piece, xor) for piece, xor in zip(pair, (2, 3))]
    out = local(
        ffn_kernel,
        out_shape=shape((groups * 2, half, width), BF16),
        in_specs=[VMEM] * (6 + 2 * len(sizes)),
        out_specs=VMEM,
        name="ffn",
    )(
        stream,
        ffn_gain.reshape(1, model_width),
        w_inner,
        near_inner,
        w_outer,
        near_outer,
        *pair,
        *others,
    )
    if not halved(share):
        padded = jnp.zeros((groups * 2, rows, width), BF16)
        out = lax.dynamic_update_slice_in_dim(padded, out, side * half, 1)
    parts = lax.all_to_all(
        out.reshape(groups * 2 * replicas, -1, width), ("hi", "lo", "rep"), 0, 0, tiled=True
    )
    parts = parts.reshape(groups, 2, replicas, -1, width).astype(F32)
    if halved(share):
        merged = local(
            merge_kernel,
            out_shape=shape((replicas, share, width), BF16),
            in_specs=[VMEM],
            out_specs=VMEM,
            name="merge",
        )(parts)
        return merged.reshape(rows, width)
    return jnp.sum(parts, axis=(0, 1)).reshape(rows, width).astype(BF16)


def solution(mesh):
    replicas, tp = mesh.shape["rep"], mesh.shape["tp"]
    split = Mesh(mesh.devices.reshape(replicas, tp // 2, 2), ("rep", "hi", "lo"))
    cols = ("hi", "lo")
    in_specs = (
        P("rep", cols),
        P(),
        P(),
        P(None, cols),
        P(None, cols),
        P(None, cols),
        P(cols, None),
        P(None, cols),
        P(cols, None),
        P(None, cols),
        P("rep", None, cols),
        P("rep", None, cols),
        P(None, "rep"),
        P(None, "rep"),
        P("rep", None),
    )
    return jax.shard_map(
        functools.partial(on_device, replicas),
        mesh=split,
        in_specs=in_specs,
        out_specs=P("rep", cols),
        check_vma=False,
    )
```
